32 devices in a mesh: dp: 8 (over y, x, core), mp: 4 (over z).
Axes of the slice: x: 2, y: 2, z: 4, core: 2. Of those that a mesh axis runs over, the one named last changes fastest.
Arguments:
- task_codes: bfloat16 [16, 128], replicated, may hold values from -6 to 6
- hyper_weight: bfloat16 [128, 196608], P(None, ('dp', 'mp')), may hold values from -0.5 to 0.5
- frozen_weight: bfloat16 [5120, 1024], P('mp'), may hold values from -0.125 to 0.125
- tokens: bfloat16 [8192, 5120], P(('dp', 'mp')), may hold values from -6 to 6
- teacher: bfloat16 [8192, 1024], P(('dp', 'mp')), may hold values from -6 to 6
- seq_slot: int32 [64], P(('dp', 'mp')), may hold values from 0 to 3, as said below
- task_share: int32 [8], replicated, may hold values from 1 to 4, as said below
- token_counts: int32 [16], replicated, may hold values from 1024 to 3071
Outputs:
- hyper_grad: float32 [128, 196608], P(None, ('dp', 'mp'))
The draws below stay inside these ranges and needn't reach their ends.
Inputs may be any that keep to these rules, and one draw needn't show every extreme that they name: Group g owns task_share[g] tasks, numbered after those of groups 0 to g - 1; the entries sum to 16; in every draw some group owns exactly 4 tasks. For sequence s of group g = s // 8, seq_slot[s] < task_share[g]; in every group some sequence names the group's last task.
All inputs are finite; a program needn't handle non-finite values.
Results may differ from the reference program's by a relative error of at most 0.012.
Values may be sent and summed in bfloat16 or wider, within the bound.
No kernel may reach another device: no remote copies, remote signals or barrier semaphores. Data moves between devices by JAX's collectives and lax.ppermute only.
A program may use at most 64 MiB of HBM per device.

```python
import math
import jax
import jax.numpy as jnp
from jax import lax

D = 5120
KV = 1024
R = 32
H = 128
TASK_GRP = 2
TPG = 4
TOK_DEV = 256
SEQ_LEN = 128
TASKS = 16
TOK_GRP = 1024
TOKENS = 8192
SEQ_GRP = 8
SEQS = 64
P_SIZE = 196608
N_DP = 8
N_MP = 4


def fraction_lookup(key):
    groups = TASKS // TASK_GRP
    base_key = jax.random.fold_in(key, 7)
    ordering = jax.random.permutation(jax.random.fold_in(base_key, 1), groups)
    heaviest = ordering[0]
    tallies = jnp.full((groups,), TASK_GRP, jnp.int32).at[heaviest].set(TPG)

    def lower_one(position, carried):
        current, remain = carried
        target = ordering[position]
        amount = jnp.minimum(remain, TASK_GRP - 1).astype(jnp.int32)
        return (current.at[target].add(-amount), remain - amount)
    tallies, remain = lax.fori_loop(1, groups, lower_one, (tallies, jnp.int32(TPG - TASK_GRP)))

    def move_one(step_index, current):
        step_key = jax.random.fold_in(base_key, 100 + step_index)
        source = jax.random.randint(jax.random.fold_in(step_key, 1), (), 0, groups, dtype=jnp.int32)
        destination = jax.random.randint(jax.random.fold_in(step_key, 2), (), 0, groups, dtype=jnp.int32)
        allowed = (current[source] > 1) & (current[destination] < TPG) & (source != heaviest) & (source != destination)
        change = allowed.astype(jnp.int32)
        return current.at[source].add(-change).at[destination].add(change)
    return lax.fori_loop(0, 4 * groups, move_one, tallies)


def draw_task_share(key, part):
    return fraction_lookup(key).astype(jnp.int32)


def draw_seq_slot(key, part):
    tallies = fraction_lookup(key)
    groups = TASKS // TASK_GRP
    owners = jnp.arange(SEQS, dtype=jnp.int32) // SEQ_GRP
    limits = tallies[owners]
    raw_bits = jax.random.randint(jax.random.fold_in(key, 11), (SEQS,), 0, 1 << 20, dtype=jnp.int32)
    slot_draw = raw_bits % limits
    marked = jax.random.randint(jax.random.fold_in(key, 13), (groups,), 0, SEQ_GRP, dtype=jnp.int32)
    is_marked = jnp.arange(SEQS, dtype=jnp.int32) % SEQ_GRP == marked[owners]
    return jnp.where(is_marked, limits - 1, slot_draw).astype(jnp.int32)


def plant(result, own_key, low, top_value):
    longest = result.shape.index(max(result.shape))
    spots = []
    for shift in (0, 1):
        where = [jax.random.randint(jax.random.fold_in(own_key, axis), (), 0, length) for axis, length in enumerate(result.shape)]
        where[longest] = (where[longest] + shift) % result.shape[longest]
        spots.append(tuple(where))
    return result.at[spots[0]].set(low).at[spots[1]].set(top_value)


def raised(values, own_key, source, target, shards_of, factor):
    def block_of(axis_at):
        return (jnp.arange(values.shape[axis_at]) // (values.shape[axis_at] // shards_of)).reshape((-1,) + (1,) * (values.ndim - 1 - axis_at))

    first = jax.random.permutation(own_key, shards_of)[block_of(target)]
    far = (block_of(target) + shards_of // 2) % shards_of
    return jnp.where((block_of(source) == first) | (block_of(source) == far), factor * values, values)


def steps_of(rng, dims, pieces, least, largest):
    level = 1.0
    for axis_at, blocks in pieces:
        draws = jax.random.uniform(jax.random.fold_in(jax.random.fold_in(rng, 6), axis_at), (blocks,), jnp.float32, least / len(pieces), largest / len(pieces))
        level = level * jnp.repeat(jnp.exp(draws), dims[axis_at] // blocks).reshape((-1,) + (1,) * (len(dims) - 1 - axis_at))
    return level


def noise(rng, extent, deviation, limit, shards=(), held_as=jnp.bfloat16):
    gain = steps_of(rng, extent, shards, -0.22, 0.18) if shards else 1.0
    result = jax.random.normal(rng, extent, jnp.float32) * deviation * gain
    return jnp.minimum(jnp.maximum(result, -limit), limit).astype(held_as)


def heavy_noise(rng, dims, width, bound, cuts, heavy, kind=jnp.bfloat16):
    entries = width * jax.random.normal(rng, dims, jnp.float32)
    if cuts:
        entries = entries * steps_of(rng, dims, cuts, -0.22, 0.18)
    return jnp.clip(raised(entries, jax.random.fold_in(rng, 3), *heavy), -bound, bound).astype(kind)


def setup_inputs(seed: int = 0) -> dict:
    key_list = jax.random.split(jax.random.key(seed), 9)
    return {
        "task_codes": noise(key_list[0], (TASKS, H), 1.0, 6.0),
        "hyper_weight": noise(key_list[1], (H, P_SIZE), H ** -0.5, 0.5, ((1, 32),)),
        "frozen_weight": heavy_noise(key_list[2], (D, KV), D ** -0.5, 0.125, ((0, 4),), (0, 1, 4, 2.0)),
        "tokens": noise(key_list[3], (TOKENS, D), 1.0, 6.0, ((0, 32),)),
        "teacher": noise(key_list[4], (TOKENS, KV), 1.0, 6.0, ((0, 32),)),
        "seq_slot": draw_seq_slot(jax.random.fold_in(key_list[8], 71), 0),
        "task_share": draw_task_share(jax.random.fold_in(key_list[8], 71), 0),
        "token_counts": plant(jax.random.randint(key_list[7], (TASKS,), 1024, 3072), jax.random.fold_in(key_list[7], 1), 1024, 3071).astype(jnp.int32),
    }


def reference(task_codes, hyper_weight, frozen_weight, tokens, teacher, seq_slot, task_share, token_counts):
    adapters = jnp.dot(task_codes, hyper_weight, preferred_element_type=jnp.float32).astype(jnp.bfloat16)
    offsets = (jnp.cumsum(task_share) - task_share).astype(jnp.int32)
    group_of = (jnp.arange(SEQS, dtype=jnp.int32) // SEQ_GRP).astype(jnp.int32)
    seq_task = (offsets[group_of] + seq_slot).astype(jnp.int32)
    counts = token_counts.astype(jnp.float32)
    task_weight = jnp.mean(counts) / counts
    shrink_factor = 1.0 / math.sqrt(D)
    rank_scale = 1.0 / math.sqrt(R)
    loss_scale = 1.0 / math.sqrt(TOK_GRP)
    seq_dev = TOK_DEV // SEQ_LEN
    blocks_all = N_DP * N_MP
    token_blocks = tokens.reshape(blocks_all, seq_dev, SEQ_LEN, D)
    teacher_blocks = teacher.reshape(blocks_all, seq_dev, SEQ_LEN, KV)
    blocks_per_task = seq_task.reshape(blocks_all, seq_dev)
    earlier = jnp.tril(jnp.ones((seq_dev, seq_dev), jnp.float32), -1)

    def one_block(accumulated, inputs):
        tokens_per_block, block_teacher, block_tasks = inputs
        chosen = jnp.take(adapters, block_tasks, axis=0).astype(jnp.float32)
        adapter_input = chosen[:, :D * R].reshape(seq_dev, D, R)
        adapter_out = chosen[:, D * R:].reshape(seq_dev, R, KV)
        flat_tokens = tokens_per_block.reshape(TOK_DEV, D)
        wide_sample_matrix = tokens_per_block.astype(jnp.float32)
        compact_factor_carry = lax.optimization_barrier((jnp.einsum('uep,upm->uem', wide_sample_matrix, adapter_input) * shrink_factor).astype(jnp.bfloat16))
        frozen_out = jnp.dot(flat_tokens, frozen_weight, preferred_element_type=jnp.float32).reshape(seq_dev, SEQ_LEN, KV)
        wide_low = compact_factor_carry.astype(jnp.float32)
        adapter_term = jnp.einsum('slr,srk->slk', wide_low, adapter_out) * rank_scale
        values = frozen_out + adapter_term
        weight = task_weight[block_tasks] * loss_scale
        value_grad = lax.optimization_barrier(((values - block_teacher.astype(jnp.float32)) * weight[:, None, None]).astype(jnp.bfloat16))
        expanded_derivative = value_grad.astype(jnp.float32)
        narrow_derivative = lax.optimization_barrier((jnp.einsum('slk,srk->slr', expanded_derivative, adapter_out) * rank_scale).astype(jnp.bfloat16))
        primary_derivative = jnp.einsum('igu,igl->iul', wide_sample_matrix, narrow_derivative.astype(jnp.float32)) * shrink_factor
        second_grad = jnp.einsum('slr,slk->srk', wide_low, expanded_derivative) * rank_scale
        per_seq = jnp.concatenate([primary_derivative.reshape(seq_dev, D * R), second_grad.reshape(seq_dev, R * KV)], axis=1)
        same_task = (block_tasks[:, None] == block_tasks[None, :]).astype(jnp.float32)
        merged_total = jnp.dot(same_task, per_seq, precision=lax.Precision.HIGHEST)
        repeated = lax.optimization_barrier(jnp.sum(same_task * earlier, axis=1)) > 0
        rounded = lax.optimization_barrier(merged_total.astype(jnp.bfloat16)).astype(jnp.float32)
        rounded = jnp.where(repeated[:, None], jnp.zeros_like(rounded), rounded)
        return (accumulated.at[block_tasks].add(rounded), None)
    adapter_grad, unused_out = lax.scan(one_block, jnp.zeros((TASKS, P_SIZE), jnp.float32), (token_blocks, teacher_blocks, blocks_per_task))
    return jnp.dot(task_codes.astype(jnp.float32).T, adapter_grad, precision=lax.Precision.HIGHEST)
```

```python
import functools
import math

import jax
import jax.numpy as jnp
from jax import lax
from jax.experimental import pallas as pl
from jax.experimental.pallas import tpu as pltpu
from jax.sharding import PartitionSpec as P

D = 5120
KV = 1024
R = 32
SEQ_LEN = 128
LANES = 128
PACK = LANES // R
A_ROWS = D * R // LANES
B_ROWS = R * KV // LANES
COL_TILES = KV // LANES
BLOCK_D = 512
BLOCK_Q = BLOCK_D // PACK
SHRINK = 1.0 / math.sqrt(D)
RANK_SCALE = 1.0 / math.sqrt(R)
F32 = jnp.float32
BF16 = jnp.bfloat16
VMEM_LIMIT = 48 * 1024 * 1024


def dot(a, b):
    return jnp.dot(a, b, preferred_element_type=F32)


def dot_nt(a, b):
    return lax.dot_general(a, b, (((1,), (1,)), ((), ())), preferred_element_type=F32)


def call(body, outs, scratch=(), n_smem=0, n_in=0, flops=0, nbytes=0, **kw):
    specs = [pl.BlockSpec(memory_space=pltpu.SMEM)] * n_smem
    specs += [pl.BlockSpec(memory_space=pltpu.VMEM)] * n_in
    out_specs = [pl.BlockSpec(memory_space=pltpu.VMEM)] * len(outs)
    return pl.pallas_call(
        body,
        out_shape=list(outs),
        in_specs=specs,
        out_specs=out_specs,
        scratch_shapes=list(scratch),
        compiler_params=pltpu.CompilerParams(vmem_limit_bytes=VMEM_LIMIT),
        cost_estimate=pl.CostEstimate(flops=flops, bytes_accessed=nbytes, transcendentals=0),
        **kw,
    )


def sds(shape, dtype):
    return jax.ShapeDtypeStruct(shape, dtype)


def xor_permute(array, axis, mask):
    return lax.ppermute(array, axis, [(i, i ^ mask) for i in range(lax.axis_size(axis))])


def adapters_kernel(tiles, task_ref, codes_ref, weight_ref, out_ref, scr):
    rows = task_ref.shape[0]
    tasks = codes_ref.shape[0]
    pick = (task_ref[...] == lax.broadcasted_iota(jnp.int32, (rows, tasks), 1)).astype(BF16)
    chosen = dot(pick, codes_ref[...]).astype(BF16)
    for k in range(tiles):
        part = dot(chosen, weight_ref[:, k * LANES : (k + 1) * LANES])
        scr[pl.ds(k, rows, stride=tiles), :] = part
    for i in range(rows):
        out_ref[i] = scr[i * tiles : (i + 1) * tiles, :].astype(BF16)


def low_rank_kernel(adapt_ref, tokens_ref, low_ref, b4_ref, tok_t_ref, scr, held):
    seqs = b4_ref.shape[0]
    if len(adapt_ref.shape) == 4:
        tiles = adapt_ref.shape[2]
        for i in range(adapt_ref.shape[0]):
            for s in range(seqs):
                held[s, i * tiles : (i + 1) * tiles, :] = adapt_ref[i, s]
        adapt_ref = held
    lane = lax.broadcasted_iota(jnp.int32, (BLOCK_D, LANES * seqs), 1)
    row = lax.broadcasted_iota(jnp.int32, (BLOCK_D, LANES * seqs), 0)
    keep = (lane % LANES) // R == row % PACK
    spread = (
        lax.broadcasted_iota(jnp.int32, (BLOCK_D, BLOCK_Q), 0) // PACK
        == lax.broadcasted_iota(jnp.int32, (BLOCK_D, BLOCK_Q), 1)
    ).astype(BF16)
    acc = jnp.zeros((tokens_ref.shape[0], LANES * seqs), F32)
    for b in range(D // BLOCK_D):
        cols = slice(b * BLOCK_D, (b + 1) * BLOCK_D)
        part = jnp.concatenate(
            [adapt_ref[s, b * BLOCK_Q : (b + 1) * BLOCK_Q, :] for s in range(seqs)], axis=1
        )
        wide = jnp.where(keep, dot(spread, part), 0.0).astype(BF16)
        block = tokens_ref[:, cols]
        acc = acc + dot(block, wide)
        tok_t_ref[cols, :] = block.T
    first = lax.broadcasted_iota(jnp.int32, (SEQ_LEN, LANES), 1) < R
    for s in range(seqs):
        z = acc[s * SEQ_LEN : (s + 1) * SEQ_LEN, s * LANES : (s + 1) * LANES]
        total = z
        for j in range(1, PACK):
            total = total + pltpu.roll(z, j * R, 1)
        low_ref[s * SEQ_LEN : (s + 1) * SEQ_LEN, :] = jnp.where(first, total * SHRINK, 0.0).astype(
            BF16
        )
        scr[...] = adapt_ref[s, A_ROWS:, :].astype(F32)
        for c in range(COL_TILES):
            piece = scr[pl.ds(c, R, stride=COL_TILES), :].astype(BF16)
            for j in range(PACK):
                b4_ref[s, j * R : (j + 1) * R, c * LANES : (c + 1) * LANES] = piece


def frozen_kernel(members, place_ref, weight_ref, own_ref, other_ref, *refs):
    pieces, (out_own, out_other) = refs[:-2], refs[-2:]
    half = out_own.shape[1]
    depth = weight_ref.shape[0]
    width = pieces[0].shape[1]
    me, core, chip = place_ref[0], place_ref[1], place_ref[2]
    rows = own_ref.shape[0]

    def both(block):
        cols = pl.ds(pl.multiple_of(block * depth, LANES), depth)
        return jnp.concatenate([own_ref[:, cols], other_ref[:, cols]], axis=0)

    first = dot(both(me), weight_ref[:, pl.ds(pl.multiple_of(core * half, LANES), half)])
    out_own[...] = first[:rows]
    out_other[...] = first[rows:]
    for k in range(1, members):
        left = both(me ^ k)
        span = slice((k - 1) * depth, k * depth)
        for m in range(0, len(pieces), 2):
            pair = range(m, min(m + 2, len(pieces)))
            right = jnp.concatenate([pieces[i][span, :] for i in pair], axis=1)
            part = dot(left, right)
            for at, i in enumerate(pair):
                cols = pl.ds(pl.multiple_of((chip ^ i) * width, LANES), width)
                out_own[:, cols] += part[:rows, at * width : (at + 1) * width]
                out_other[:, cols] += part[rows:, at * width : (at + 1) * width]


def backward_kernel(
    place_ref, scale_ref, mine_ref, theirs_ref, teacher_ref, low_ref, b4_ref, tok_t_ref, out_ref,
    values, spaced, grads,
):
    seqs = b4_ref.shape[0]
    half = mine_ref.shape[1]
    core = place_ref[1]
    values[:, pl.ds(pl.multiple_of(core * half, LANES), half)] = mine_ref[...]
    values[:, pl.ds(pl.multiple_of((1 - core) * half, LANES), half)] = theirs_ref[...]
    blocks = []
    for s in range(seqs):
        rows = slice(s * SEQ_LEN, (s + 1) * SEQ_LEN)
        low = low_ref[rows, :]
        b4 = b4_ref[s]
        error = values[rows, :] + dot(low, b4) * RANK_SCALE - teacher_ref[rows, :].astype(F32)
        value_grad = (error * scale_ref[s]).astype(BF16)
        blocks.append((dot_nt(value_grad, b4) * RANK_SCALE).astype(BF16))
        second = dot(low.T, value_grad)[:R] * RANK_SCALE
        for c in range(COL_TILES):
            spaced[pl.ds(c, R, stride=COL_TILES), :] = second[:, c * LANES : (c + 1) * LANES]
        grads[s, A_ROWS:, :] = spaced[...].astype(BF16)
    zero = jnp.zeros_like(blocks[0])
    low_grad = jnp.concatenate(
        [
            jnp.concatenate([blocks[s] if s == i else zero for i in range(seqs)], axis=1)
            for s in range(seqs)
        ],
        axis=0,
    )
    lane = lax.broadcasted_iota(jnp.int32, (BLOCK_D, LANES * seqs), 1)
    row = lax.broadcasted_iota(jnp.int32, (BLOCK_D, LANES * seqs), 0)
    keep = (lane % LANES) // R == row % PACK
    merge = (
        lax.broadcasted_iota(jnp.int32, (BLOCK_Q, BLOCK_D), 1) // PACK
        == lax.broadcasted_iota(jnp.int32, (BLOCK_Q, BLOCK_D), 0)
    ).astype(BF16)
    for b in range(D // BLOCK_D):
        full = dot(tok_t_ref[b * BLOCK_D : (b + 1) * BLOCK_D, :], low_grad)
        kept = jnp.where(keep, full * SHRINK, 0.0).astype(BF16)
        merged = dot(merge, kept).astype(BF16)
        for s in range(seqs):
            grads[s, b * BLOCK_Q : (b + 1) * BLOCK_Q, :] = merged[:, s * LANES : (s + 1) * LANES]
    store_grads(grads, out_ref)


def store_grads(grads, out_ref):
    if len(out_ref.shape) == 3:
        out_ref[...] = grads[...]
        return
    tiles = out_ref.shape[2]
    for i in range(out_ref.shape[0]):
        for s in range(out_ref.shape[1]):
            out_ref[i, s] = grads[s, i * tiles : (i + 1) * tiles, :]


def hyper_kernel(codes_t_ref, grads_ref, out_ref, scr):
    devices, seqs, tiles, _ = grads_ref.shape
    rows = devices * seqs
    for i in range(devices):
        for s in range(seqs):
            at = (i * seqs + s) * tiles
            scr[at : at + tiles, :] = grads_ref[i, s].astype(F32)
    codes_t = codes_t_ref[...]
    for k in range(tiles):
        part = scr[pl.ds(k, rows, stride=tiles), :].astype(BF16)
        out_ref[:, k * LANES : (k + 1) * LANES] = dot(codes_t, part)


def shards(
    task_codes, hyper_weight, frozen_weight, tokens, teacher, seq_slot, task_share, token_counts
):
    groups = lax.axis_size("dp")
    members = lax.axis_size("mp")
    devices = groups * members
    chips = groups // 2
    tok_dev = tokens.shape[0]
    seqs = seq_slot.shape[0]
    depth = frozen_weight.shape[0]
    tiles = hyper_weight.shape[1] // LANES
    rows = A_ROWS + B_ROWS
    n_tasks, width_h = task_codes.shape
    loss_scale = 1.0 / math.sqrt(tok_dev * members)
    me_dp, me_mp = lax.axis_index("dp"), lax.axis_index("mp")
    core, chip = me_dp % 2, me_dp // 2
    place = jnp.stack([me_mp, core, chip]).astype(jnp.int32)
    half = KV // 2
    width = half // chips
    whole_tiles = tiles % 16 == 0

    chunk = lax.dynamic_slice_in_dim(frozen_weight, core * half + chip * width, width, 1)
    arrived = jnp.concatenate(
        [xor_permute(chunk, "mp", k) for k in range(1, members)], axis=0
    )
    other_tokens = xor_permute(tokens, "dp", 1)

    slots = lax.all_to_all(
        jnp.broadcast_to(seq_slot[None], (devices, seqs)), ("dp", "mp"), 0, 0, tiled=True
    ).reshape(-1)
    offsets = jnp.cumsum(task_share) - task_share
    task_of = jnp.repeat(offsets, members * seqs) + slots
    codes_t = jnp.dot(
        task_codes.T, (jnp.arange(n_tasks)[:, None] == task_of[None, :]).astype(BF16),
        preferred_element_type=F32,
    ).astype(BF16)
    counts = token_counts.astype(F32)
    task_weight = jnp.mean(counts) / counts
    own_task = jnp.take(offsets, me_dp) + seq_slot
    scale = jnp.take(task_weight, own_task) * loss_scale

    held = {0: arrived}
    middle = arrived.shape[0] // 2
    for m in range(1, chips):
        low_bit, high_bit = m & -m, 1 << (m.bit_length() - 1)
        if low_bit == high_bit:
            held[m] = xor_permute(arrived, "dp", m << 1)
        else:
            held[m] = jnp.concatenate(
                [
                    xor_permute(held[m ^ high_bit][:middle], "dp", high_bit << 1),
                    xor_permute(held[m ^ low_bit][middle:], "dp", low_bit << 1),
                ],
                axis=0,
            )

    sent = call(
        functools.partial(adapters_kernel, tiles),
        [sds((devices * seqs, tiles, LANES), BF16)],
        scratch=[pltpu.VMEM((devices * seqs * tiles, LANES), F32)],
        n_in=3,
        flops=2 * devices * seqs * hyper_weight.size,
        nbytes=4 * hyper_weight.size,
    )(task_of[:, None], task_codes, hyper_weight)[0]
    adapt = lax.all_to_all(
        sent.reshape(devices, seqs, tiles, LANES), ("dp", "mp"), 0, 0, tiled=True
    )
    if not whole_tiles:
        adapt = adapt.transpose(1, 0, 2, 3).reshape(seqs, rows, LANES)
    low, b4, tok_t = call(
        low_rank_kernel,
        [
            sds((tok_dev, LANES), BF16),
            sds((seqs, LANES, KV), BF16),
            sds((D, tok_dev), BF16),
        ],
        scratch=[pltpu.VMEM((B_ROWS, LANES), F32), pltpu.VMEM((seqs, rows, LANES), BF16)],
        n_in=2,
        flops=4 * tokens.size * LANES * seqs,
        nbytes=4 * tokens.size + 4 * seqs * rows * LANES,
    )(adapt, tokens)

    if width % LANES == 0 and depth % LANES == 0:
        mine, theirs = call(
            functools.partial(frozen_kernel, members),
            [sds((tok_dev, half), F32)] * 2,
            n_smem=1,
            n_in=3 + chips,
            flops=4 * tokens.size * half,
            nbytes=4 * tokens.size + 2 * D * half,
        )(place, frozen_weight, tokens, other_tokens, *[held[m] for m in range(chips)])
    else:
        own_half = lax.dynamic_slice_in_dim(frozen_weight, core * half, half, 1)
        moved = jnp.stack([held[m].reshape(members - 1, depth, width) for m in range(chips)], 1)
        moved = jnp.take(moved, jnp.arange(chips) ^ chip, axis=1)
        moved = moved.transpose(0, 2, 1, 3).reshape(members - 1, depth, half)
        blocks = jnp.concatenate([own_half[None], moved], axis=0)
        weight = jnp.take(blocks, jnp.arange(members) ^ me_mp, axis=0).reshape(D, half)
        mine = jnp.dot(tokens, weight, preferred_element_type=F32)
        theirs = jnp.dot(other_tokens, weight, preferred_element_type=F32)
    received = xor_permute(theirs, "dp", 1)

    split = (devices, seqs, tiles, LANES)
    grads = call(
        backward_kernel,
        [sds(split if whole_tiles else (seqs, rows, LANES), BF16)],
        scratch=[
            pltpu.VMEM((tok_dev, KV), F32),
            pltpu.VMEM((B_ROWS, LANES), F32),
            pltpu.VMEM((seqs, rows, LANES), BF16),
        ],
        n_smem=2,
        n_in=6,
        flops=4 * tokens.size * LANES * seqs,
        nbytes=4 * tokens.size,
    )(place, scale, mine, received, teacher, low, b4, tok_t)[0]
    if not whole_tiles:
        grads = grads.reshape(seqs, devices, tiles, LANES).transpose(1, 0, 2, 3)
    routed = lax.all_to_all(grads, ("dp", "mp"), 0, 0, tiled=True)
    step = 16 if whole_tiles else tiles
    return pl.pallas_call(
        hyper_kernel,
        grid=(tiles // step,),
        out_shape=sds((width_h, tiles * LANES), F32),
        in_specs=[
            pl.BlockSpec((width_h, devices * seqs), lambda i: (0, 0)),
            pl.BlockSpec((devices, seqs, step, LANES), lambda i: (0, 0, i, 0)),
        ],
        out_specs=pl.BlockSpec((width_h, step * LANES), lambda i: (0, i)),
        scratch_shapes=[pltpu.VMEM((devices * seqs * step, LANES), F32)],
        compiler_params=pltpu.CompilerParams(vmem_limit_bytes=VMEM_LIMIT),
    )(codes_t, routed)


def solution(mesh):
    placed = (
        P(),
        P(None, ("dp", "mp")),
        P("mp", None),
        P(("dp", "mp"), None),
        P(("dp", "mp"), None),
        P(("dp", "mp")),
        P(),
        P(),
    )
    return jax.shard_map(
        shards, mesh=mesh, in_specs=placed, out_specs=P(None, ("dp", "mp")), check_vma=False
    )
```

```python
import functools
import math

import jax
import jax.numpy as jnp
from jax import lax
from jax.experimental import pallas as pl
from jax.experimental.pallas import tpu as pltpu
from jax.sharding import PartitionSpec as P

D = 5120
KV = 1024
R = 32
TPG = 4
SEQ_LEN = 128
LANES = 128
PACK = LANES // R
SLOT_ROWS = 16
A_ROWS = D * R // LANES
B_ROWS = R * KV // LANES
COL_TILES = KV // LANES
BLOCK_D = 512
BLOCK_Q = BLOCK_D // PACK
SHRINK = 1.0 / math.sqrt(D)
RANK_SCALE = 1.0 / math.sqrt(R)
F32 = jnp.float32
BF16 = jnp.bfloat16
VMEM_LIMIT = 16 * 1024 * 1024


def dot(a, b):
    return jnp.dot(a, b, preferred_element_type=F32)


def dot_nt(a, b):
    return lax.dot_general(a, b, (((1,), (1,)), ((), ())), preferred_element_type=F32)


def call(body, outs, scratch=(), n_smem=0, n_in=0, flops=0, nbytes=0, **kw):
    specs = [pl.BlockSpec(memory_space=pltpu.SMEM)] * n_smem
    specs += [pl.BlockSpec(memory_space=pltpu.VMEM)] * n_in
    out_specs = [pl.BlockSpec(memory_space=pltpu.VMEM)] * len(outs)
    return pl.pallas_call(
        body,
        out_shape=list(outs),
        in_specs=specs,
        out_specs=out_specs,
        scratch_shapes=list(scratch),
        compiler_params=pltpu.CompilerParams(vmem_limit_bytes=VMEM_LIMIT),
        cost_estimate=pl.CostEstimate(flops=flops, bytes_accessed=nbytes, transcendentals=0),
        **kw,
    )


def sds(shape, dtype):
    return jax.ShapeDtypeStruct(shape, dtype)


def xor_permute(array, axis, mask):
    return lax.ppermute(array, axis, [(i, i ^ mask) for i in range(lax.axis_size(axis))])


def chunk_kernel(place_ref, slot_ref, weight_ref, near_ref, top_ref, bottom_ref, sems):
    depth = weight_ref.shape[0]
    width = near_ref.shape[1]
    mid = depth // 2
    half = weight_ref.shape[1] // 2
    at = pl.ds(pl.multiple_of(place_ref[1] * half + place_ref[2] * width, LANES), width)
    copies = [
        pltpu.make_async_copy(
            weight_ref.at[pl.ds(first, size), at], out.at[pl.ds(0, size), :], sems.at[i]
        )
        for i, (first, size, out) in enumerate(
            [(0, depth, near_ref), (0, mid, top_ref), (mid, mid, bottom_ref)]
        )
    ]
    for copy in copies:
        copy.start()
    row = lax.broadcasted_iota(jnp.int32, (SLOT_ROWS, width), 0)
    note = jnp.zeros((SLOT_ROWS, width), jnp.int32)
    for s in range(slot_ref.shape[0]):
        note = jnp.where(row == s, slot_ref[s], note)
    note = note.astype(F32).astype(BF16)
    near_ref[depth:, :] = note
    top_ref[mid:, :] = note
    bottom_ref[mid:, :] = note
    for copy in copies:
        copy.wait()


def adapters_kernel(tiles, share_ref, codes_ref, weight_ref, out_ref, scr):
    groups, tpg = out_ref.shape[:2]
    rows = groups * tpg
    tasks = codes_ref.shape[0]
    row = lax.broadcasted_iota(jnp.int32, (rows, 1), 0)
    group, task = row // tpg, row % tpg
    live = jnp.zeros((rows, 1), jnp.int32)
    for g in range(groups):
        task = task + jnp.where(group > g, share_ref[g], 0)
        live = live + jnp.where(group == g, share_ref[g], 0)
    task = jnp.where(row % tpg < live, task, -1)
    pick = (task == lax.broadcasted_iota(jnp.int32, (rows, tasks), 1)).astype(BF16)
    chosen = dot(pick, codes_ref[...]).astype(BF16)
    for k in range(tiles):
        part = dot(chosen, weight_ref[:, k * LANES : (k + 1) * LANES])
        scr[pl.ds(k, rows, stride=tiles), :] = part
    for g in range(groups):
        for i in range(tpg):
            at = (g * tpg + i) * tiles
            out_ref[g, i] = scr[at : at + tiles, :].astype(BF16)


def choose_kernel(n_smem, n, *refs):
    slot_refs, got_ref, out_refs = refs[:n], refs[n], refs[n + 1 :]
    for at, (slots, out) in enumerate(zip(slot_refs, out_refs)):
        if at >= n_smem:
            rows = slots.shape[0]
            notes = slots[rows - SLOT_ROWS :, :].astype(F32)
        for s in range(out.shape[1]):
            if at < n_smem:
                slot = slots[s]
            else:
                slot = jnp.max(notes[s : s + 1, :].astype(jnp.int32))
            out[:, s] = got_ref[:, slot]


def codes_kernel(group_seqs, share_ref, slots_ref, codes_ref, out_ref):
    rows = slots_ref.shape[0]
    task = slots_ref[...]
    group = lax.broadcasted_iota(jnp.int32, (rows, 1), 0) // group_seqs
    for g in range(share_ref.shape[0] - 1):
        task = task + jnp.where(group > g, share_ref[g], 0)
    tasks = codes_ref.shape[0]
    pick = (task == lax.broadcasted_iota(jnp.int32, (rows, tasks), 1)).astype(BF16)
    out_ref[...] = dot(pick, codes_ref[...]).T.astype(BF16)


def low_rank_kernel(n, place_ref, *refs):
    adapt_refs, (tokens_ref, low_ref, b4_ref, tok_t_ref, scr, held) = refs[:n], refs[n:]
    seqs = b4_ref.shape[0]
    adapt_ref = adapt_refs[0]
    if len(adapt_ref.shape) == 4:
        groups, _, tiles, _ = adapt_ref.shape
        for k, part in enumerate(adapt_refs):
            for g in range(groups):
                at = pl.multiple_of((g * n + (place_ref[0] ^ k)) * tiles, 16)
                for s in range(seqs):
                    held[s, pl.ds(at, tiles), :] = part[g, s]
        adapt_ref = held
    lane = lax.broadcasted_iota(jnp.int32, (BLOCK_D, LANES * seqs), 1)
    row = lax.broadcasted_iota(jnp.int32, (BLOCK_D, LANES * seqs), 0)
    keep = (lane % LANES) // R == row % PACK
    spread = (
        lax.broadcasted_iota(jnp.int32, (BLOCK_D, BLOCK_Q), 0) // PACK
        == lax.broadcasted_iota(jnp.int32, (BLOCK_D, BLOCK_Q), 1)
    ).astype(BF16)
    acc = jnp.zeros((tokens_ref.shape[0], LANES * seqs), F32)
    for b in range(D // BLOCK_D):
        cols = slice(b * BLOCK_D, (b + 1) * BLOCK_D)
        part = jnp.concatenate(
            [adapt_ref[s, b * BLOCK_Q : (b + 1) * BLOCK_Q, :] for s in range(seqs)], axis=1
        )
        wide = jnp.where(keep, dot(spread, part), 0.0).astype(BF16)
        block = tokens_ref[:, cols]
        acc = acc + dot(block, wide)
        tok_t_ref[cols, :] = block.T
    first = lax.broadcasted_iota(jnp.int32, (SEQ_LEN, LANES), 1) < R
    for s in range(seqs):
        z = acc[s * SEQ_LEN : (s + 1) * SEQ_LEN, s * LANES : (s + 1) * LANES]
        total = z
        for j in range(1, PACK):
            total = total + pltpu.roll(z, j * R, 1)
        low_ref[s * SEQ_LEN : (s + 1) * SEQ_LEN, :] = jnp.where(first, total * SHRINK, 0.0).astype(
            BF16
        )
        scr[...] = adapt_ref[s, A_ROWS:, :].astype(F32)
        for c in range(COL_TILES):
            piece = scr[pl.ds(c, R, stride=COL_TILES), :].astype(BF16)
            for j in range(PACK):
                b4_ref[s, j * R : (j + 1) * R, c * LANES : (c + 1) * LANES] = piece


def frozen_kernel(n_tok, depth, own, layout, has_acc, place_ref, *refs):
    refs = iter(refs)
    token_refs = [next(refs) for _ in range(n_tok)]
    weight_ref = next(refs) if own else None
    sets = [
        ([[next(refs) for _ in range(n)] for n in counts], segments) for counts, segments in layout
    ]
    accs = [next(refs) for _ in range(n_tok)] if has_acc else [None] * n_tok
    outs = list(refs)
    me, core, chip = place_ref[0], place_ref[1], place_ref[2]
    half = outs[0].shape[1]
    width = sets[0][0][0][0].shape[1]
    chips = len(sets[0][0])

    def cols(k, first, size):
        return pl.ds(pl.multiple_of((me ^ k) * depth + first, LANES), size)

    for tok, acc, out in zip(token_refs, accs, outs):
        if own:
            block = weight_ref[:, pl.ds(pl.multiple_of(core * half, LANES), half)]
            out[...] = dot(tok[:, cols(0, 0, depth)], block)
        else:
            out[...] = acc[...]
        for m in range(0, chips, 2):
            pair = range(m, min(m + 2, chips))
            total = None
            for pieces, segments in sets:
                at = 0
                for k, first, size in segments:
                    parts = []
                    for i in pair:
                        n = pieces[i][0].shape[0]
                        piece, row = (pieces[i][0], at) if at < n else (pieces[i][1], at - n)
                        parts.append(piece[row : row + size, :])
                    part = dot(tok[:, cols(k, first, size)], jnp.concatenate(parts, axis=1))
                    total = part if total is None else total + part
                    at += size
            for at, i in enumerate(pair):
                where = pl.ds(pl.multiple_of((chip ^ i) * width, LANES), width)
                out[:, where] += total[:, at * width : (at + 1) * width]


def frozen_call(place, depth, half, tokens, weight, sets, accs):
    rows = tokens[0].shape[0]
    layout = [([len(x) for x in pieces], segments) for pieces, segments in sets]
    flat = [x for pieces, _ in sets for piece in pieces for x in piece]
    deep = sum(size for _, segments in sets for _, _, size in segments)
    deep += 0 if weight is None else depth
    weights = [] if weight is None else [weight]
    return call(
        functools.partial(
            frozen_kernel, len(tokens), depth, weight is not None, layout, bool(accs)
        ),
        [sds((rows, half), F32)] * len(tokens),
        n_smem=1,
        n_in=len(tokens) + len(weights) + len(flat) + len(accs),
        flops=2 * rows * half * deep * len(tokens),
        nbytes=2 * deep * half + 4 * rows * half * len(tokens),
    )(place, *tokens, *weights, *flat, *accs)


def backward_kernel(
    loss_scale, place_ref, share_ref, slot_ref, counts_ref, mine_ref, theirs_ref, teacher_ref, low_ref, b4_ref, tok_t_ref, out_ref,
    values, spaced, grads,
):
    seqs = b4_ref.shape[0]
    half = mine_ref.shape[1]
    core, group = place_ref[1], place_ref[3]
    n_tasks = counts_ref.shape[0]
    first_task = jnp.int32(0)
    for g in range(share_ref.shape[0]):
        first_task = first_task + jnp.where(g < group, share_ref[g], 0)
    all_counts = counts_ref[0]
    for t in range(1, n_tasks):
        all_counts = all_counts + counts_ref[t]
    values[:, pl.ds(pl.multiple_of(core * half, LANES), half)] = mine_ref[...]
    values[:, pl.ds(pl.multiple_of((1 - core) * half, LANES), half)] = theirs_ref[...]
    blocks = []
    for s in range(seqs):
        rows = slice(s * SEQ_LEN, (s + 1) * SEQ_LEN)
        low = low_ref[rows, :]
        b4 = b4_ref[s]
        error = values[rows, :] + dot(low, b4) * RANK_SCALE - teacher_ref[rows, :].astype(F32)
        count = jnp.full((1, KV), counts_ref[first_task + slot_ref[s]], jnp.int32).astype(F32)
        mean = jnp.full((1, KV), all_counts, jnp.int32).astype(F32) / n_tasks
        value_grad = (error * (mean / count * loss_scale)).astype(BF16)
        blocks.append((dot_nt(value_grad, b4) * RANK_SCALE).astype(BF16))
        second = dot(low.T, value_grad)[:R] * RANK_SCALE
        for c in range(COL_TILES):
            spaced[pl.ds(c, R, stride=COL_TILES), :] = second[:, c * LANES : (c + 1) * LANES]
        grads[s, A_ROWS:, :] = spaced[...].astype(BF16)
    zero = jnp.zeros_like(blocks[0])
    low_grad = jnp.concatenate(
        [
            jnp.concatenate([blocks[s] if s == i else zero for i in range(seqs)], axis=1)
            for s in range(seqs)
        ],
        axis=0,
    )
    lane = lax.broadcasted_iota(jnp.int32, (BLOCK_D, LANES * seqs), 1)
    row = lax.broadcasted_iota(jnp.int32, (BLOCK_D, LANES * seqs), 0)
    keep = (lane % LANES) // R == row % PACK
    merge = (
        lax.broadcasted_iota(jnp.int32, (BLOCK_Q, BLOCK_D), 1) // PACK
        == lax.broadcasted_iota(jnp.int32, (BLOCK_Q, BLOCK_D), 0)
    ).astype(BF16)
    for b in range(D // BLOCK_D):
        full = dot(tok_t_ref[b * BLOCK_D : (b + 1) * BLOCK_D, :], low_grad)
        kept = jnp.where(keep, full * SHRINK, 0.0).astype(BF16)
        merged = dot(merge, kept).astype(BF16)
        for s in range(seqs):
            grads[s, b * BLOCK_Q : (b + 1) * BLOCK_Q, :] = merged[:, s * LANES : (s + 1) * LANES]
    store_grads(grads, out_ref)


def store_grads(grads, out_ref):
    if len(out_ref.shape) == 3:
        out_ref[...] = grads[...]
        return
    tiles = out_ref.shape[2]
    for i in range(out_ref.shape[0]):
        for s in range(out_ref.shape[1]):
            out_ref[i, s] = grads[s, i * tiles : (i + 1) * tiles, :]


def hyper_kernel(codes_t_ref, grads_ref, out_ref, scr):
    devices, seqs, tiles, _ = grads_ref.shape
    rows = devices * seqs
    for i in range(devices):
        for s in range(seqs):
            at = (i * seqs + s) * tiles
            scr[at : at + tiles, :] = grads_ref[i, s].astype(F32)
    codes_t = codes_t_ref[...]
    for k in range(tiles):
        part = scr[pl.ds(k, rows, stride=tiles), :].astype(BF16)
        out_ref[:, k * LANES : (k + 1) * LANES] = dot(codes_t, part)


def tied(*groups):
    return lax.optimization_barrier(groups)


def shards(
    task_codes, hyper_weight, frozen_weight, tokens, teacher, seq_slot, task_share, token_counts
):
    groups = lax.axis_size("dp")
    members = lax.axis_size("mp")
    devices = groups * members
    chips = groups // 2
    tok_dev = tokens.shape[0]
    seqs = seq_slot.shape[0]
    depth = frozen_weight.shape[0]
    tiles = hyper_weight.shape[1] // LANES
    rows = A_ROWS + B_ROWS
    width_h = task_codes.shape[1]
    loss_scale = 1.0 / math.sqrt(tok_dev * members)
    me_dp, me_mp = lax.axis_index("dp"), lax.axis_index("mp")
    core, chip = me_dp % 2, me_dp // 2
    place = jnp.stack([me_mp, core, chip, me_dp]).astype(jnp.int32)
    half = KV // 2
    width = half // chips
    whole_tiles = tiles % 16 == 0

    other_tokens = xor_permute(tokens, "dp", 1)
    mid = depth // 2
    fits = width % LANES == 0 and mid % LANES == 0 and members == 4
    near_rows = [(1, 0, mid), (1, mid, mid)]
    if fits:
        near, top, bottom = pl.pallas_call(
            chunk_kernel,
            in_specs=[pl.BlockSpec(memory_space=pltpu.SMEM)] * 2
            + [pl.BlockSpec(memory_space=pl.ANY)],
            out_specs=[pl.BlockSpec(memory_space=pltpu.VMEM)] * 3,
            out_shape=[sds((n + SLOT_ROWS, width), BF16) for n in (depth, mid, mid)],
            scratch_shapes=[pltpu.SemaphoreType.DMA((3,))],
            compiler_params=pltpu.CompilerParams(vmem_limit_bytes=VMEM_LIMIT),
        )(place, seq_slot, frozen_weight)
        near = xor_permute(near, "mp", 1)
        top = xor_permute(top, "mp", 2)
        bottom = xor_permute(bottom, "mp", 3)
        far = jnp.concatenate([top[:mid], bottom[:mid]], axis=0)
        rest = jnp.concatenate([far, xor_permute(far, "mp", 1)], axis=0)
        rest_rows = [(2, 0, mid), (3, mid, mid), (3, 0, mid), (2, mid, mid)]
        member_slots, n_smem = [seq_slot, near, top, bottom], 1
    else:
        chunk = lax.dynamic_slice_in_dim(frozen_weight, core * half + chip * width, width, 1)
        near = xor_permute(chunk, "mp", 1)
        rest = jnp.concatenate(
            [xor_permute(chunk, "mp", k) for k in range(2, members)], axis=0
        )
        rest_rows = [(k, at, mid) for k in range(2, members) for at in (0, mid)]
        member_slots = [seq_slot] + [xor_permute(seq_slot, "mp", k) for k in range(1, members)]
        n_smem = members

    def halves(parts):
        if len(parts) == 2:
            return parts
        middle = parts[0].shape[0] // (2 * mid) * mid
        return [parts[0][:middle], parts[0][middle:]]

    def direct(block):
        held = {0: [block]}
        for m in range(1, chips):
            if m & (m - 1) == 0:
                held[m] = [xor_permute(block, "dp", m << 1)]
        return held

    def forwarded(held):
        for m in range(1, chips):
            if m not in held:
                low_bit, high_bit = m & -m, 1 << (m.bit_length() - 1)
                held[m] = [
                    xor_permute(halves(held[m ^ high_bit])[0], "dp", high_bit << 1),
                    xor_permute(halves(held[m ^ low_bit])[1], "dp", low_bit << 1),
                ]
        return [held[m] for m in range(chips)]

    near_pieces = forwarded(direct(near))

    split = (groups, TPG, tiles, LANES)
    sent = call(
        functools.partial(adapters_kernel, tiles),
        [sds(split, BF16)],
        scratch=[pltpu.VMEM((groups * TPG * tiles, LANES), F32)],
        n_smem=1,
        n_in=2,
        flops=2 * groups * TPG * hyper_weight.size,
        nbytes=4 * hyper_weight.size,
    )(task_share, task_codes, hyper_weight)[0]
    got = lax.all_to_all(sent, "dp", 0, 0, tiled=True)
    chosen = call(
        functools.partial(choose_kernel, n_smem, members),
        [sds((groups, seqs, tiles, LANES), BF16)] * members,
        n_smem=n_smem,
        n_in=members - n_smem + 1,
        nbytes=8 * hyper_weight.size,
    )(*member_slots, got)
    near_pieces, rest, chosen = tied(near_pieces, rest, chosen)
    adapt = [chosen[0]] + [xor_permute(chosen[k], "mp", k) for k in range(1, members)]
    if not whole_tiles:
        adapt = jnp.take(jnp.stack(adapt), jnp.arange(members) ^ me_mp, axis=0)
        adapt = [adapt.transpose(2, 1, 0, 3, 4).reshape(seqs, rows, LANES)]

    rest_held = direct(rest)
    accs = []
    if fits:
        accs = frozen_call(
            place, depth, half, [tokens, other_tokens], frozen_weight, [(near_pieces, near_rows)], []
        )
    later_slot, accs = tied(seq_slot, accs)
    slots = lax.all_to_all(
        jnp.broadcast_to(later_slot[None], (devices, seqs)), ("dp", "mp"), 0, 0, tiled=True
    )
    codes_t = call(
        functools.partial(codes_kernel, members * seqs),
        [sds((width_h, devices * seqs), BF16)],
        n_smem=1,
        n_in=2,
    )(task_share, slots.reshape(-1, 1), task_codes)[0]
    rest_held, accs, codes_t, adapt = tied(rest_held, accs, codes_t, adapt)
    rest_pieces = forwarded(rest_held)

    low, b4, tok_t = call(
        functools.partial(low_rank_kernel, len(adapt)),
        [
            sds((tok_dev, LANES), BF16),
            sds((seqs, LANES, KV), BF16),
            sds((D, tok_dev), BF16),
        ],
        scratch=[pltpu.VMEM((B_ROWS, LANES), F32), pltpu.VMEM((seqs, rows, LANES), BF16)],
        n_smem=1,
        n_in=len(adapt) + 1,
        flops=4 * tokens.size * LANES * seqs,
        nbytes=4 * tokens.size + 4 * seqs * rows * LANES,
    )(place, *adapt, tokens)

    if fits:
        accs, low = tied(accs, low)
        late = [(rest_pieces, rest_rows)]
        theirs = frozen_call(place, depth, half, [other_tokens], None, late, accs[1:])[0]
        mine = frozen_call(place, depth, half, [tokens], None, late, accs[:1])[0]
    else:
        own_half = lax.dynamic_slice_in_dim(frozen_weight, core * half, half, 1)
        order = jnp.arange(chips) ^ chip
        found = {(0, 0): own_half[:mid], (0, mid): own_half[mid:]}
        for pieces, segments in ((near_pieces, near_rows), (rest_pieces, rest_rows)):
            joined = jnp.stack([jnp.concatenate(x, axis=0) for x in pieces])
            joined = jnp.take(joined, order, axis=0).transpose(1, 0, 2).reshape(-1, half)
            for at, (k, first, size) in enumerate(segments):
                found[k, first] = joined[at * size : (at + 1) * size]
        blocks = jnp.stack(
            [jnp.concatenate([found[k, 0], found[k, mid]], axis=0) for k in range(members)]
        )
        weight = jnp.take(blocks, jnp.arange(members) ^ me_mp, axis=0).reshape(D, half)
        mine = jnp.dot(tokens, weight, preferred_element_type=F32)
        theirs = jnp.dot(other_tokens, weight, preferred_element_type=F32)
    received = xor_permute(theirs, "dp", 1)

    split = (devices, seqs, tiles, LANES)
    grads = call(
        functools.partial(backward_kernel, loss_scale),
        [sds(split if whole_tiles else (seqs, rows, LANES), BF16)],
        scratch=[
            pltpu.VMEM((tok_dev, KV), F32),
            pltpu.VMEM((B_ROWS, LANES), F32),
            pltpu.VMEM((seqs, rows, LANES), BF16),
        ],
        n_smem=4,
        n_in=6,
        flops=4 * tokens.size * LANES * seqs,
        nbytes=4 * tokens.size,
    )(place, task_share, seq_slot, token_counts, mine, received, teacher, low, b4, tok_t)[0]
    if not whole_tiles:
        grads = grads.reshape(seqs, devices, tiles, LANES).transpose(1, 0, 2, 3)
    routed = lax.all_to_all(grads, ("dp", "mp"), 0, 0, tiled=True)
    step = 16 if whole_tiles else tiles
    return pl.pallas_call(
        hyper_kernel,
        grid=(tiles // step,),
        out_shape=sds((width_h, tiles * LANES), F32),
        in_specs=[
            pl.BlockSpec((width_h, devices * seqs), lambda i: (0, 0)),
            pl.BlockSpec((devices, seqs, step, LANES), lambda i: (0, 0, i, 0)),
        ],
        out_specs=pl.BlockSpec((width_h, step * LANES), lambda i: (0, i)),
        scratch_shapes=[pltpu.VMEM((devices * seqs * step, LANES), F32)],
        compiler_params=pltpu.CompilerParams(vmem_limit_bytes=VMEM_LIMIT),
    )(codes_t, routed)


def solution(mesh):
    placed = (
        P(),
        P(None, ("dp", "mp")),
        P("mp", None),
        P(("dp", "mp"), None),
        P(("dp", "mp"), None),
        P(("dp", "mp")),
        P(),
        P(),
    )
    return jax.shard_map(
        shards, mesh=mesh, in_specs=placed, out_specs=P(None, ("dp", "mp")), check_vma=False
    )
```

```python
import functools
import math

import jax
import jax.numpy as jnp
from jax import lax
from jax.experimental import pallas as pl
from jax.experimental.pallas import tpu as pltpu
from jax.sharding import PartitionSpec as P

D = 5120
KV = 1024
R = 32
TPG = 4
SEQ_LEN = 128
LANES = 128
PACK = LANES // R
SLOT_ROWS = 16
A_ROWS = D * R // LANES
B_ROWS = R * KV // LANES
COL_TILES = KV // LANES
BLOCK_D = 512
BLOCK_Q = BLOCK_D // PACK
SHRINK = 1.0 / math.sqrt(D)
RANK_SCALE = 1.0 / math.sqrt(R)
F32 = jnp.float32
BF16 = jnp.bfloat16
VMEM_LIMIT = 16 * 1024 * 1024
ALL_VMEM = 56 * 1024 * 1024


def dot(a, b):
    return jnp.dot(a, b, preferred_element_type=F32)


def dot_nt(a, b):
    return lax.dot_general(a, b, (((1,), (1,)), ((), ())), preferred_element_type=F32)


def call(body, outs, scratch=(), n_smem=0, n_in=0, flops=0, nbytes=0, **kw):
    specs = [pl.BlockSpec(memory_space=pltpu.SMEM)] * n_smem
    specs += [pl.BlockSpec(memory_space=pltpu.VMEM)] * n_in
    out_specs = [pl.BlockSpec(memory_space=pltpu.VMEM)] * len(outs)
    return pl.pallas_call(
        body,
        out_shape=list(outs),
        in_specs=specs,
        out_specs=out_specs,
        scratch_shapes=list(scratch),
        compiler_params=pltpu.CompilerParams(vmem_limit_bytes=VMEM_LIMIT),
        cost_estimate=pl.CostEstimate(flops=flops, bytes_accessed=nbytes, transcendentals=0),
        **kw,
    )


def sds(shape, dtype):
    return jax.ShapeDtypeStruct(shape, dtype)


def xor_permute(array, axis, mask):
    return lax.ppermute(array, axis, [(i, i ^ mask) for i in range(lax.axis_size(axis))])


def chunk_kernel(place_ref, slot_hbm, weight_ref, near_ref, top_ref, bottom_ref, slot_ref, sems):
    depth = weight_ref.shape[0]
    width = near_ref.shape[1]
    mid = depth // 2
    half = weight_ref.shape[1] // 2
    at = pl.ds(pl.multiple_of(place_ref[1] * half + place_ref[2] * width, LANES), width)
    copies = [
        pltpu.make_async_copy(
            weight_ref.at[pl.ds(first, size), at], out.at[pl.ds(0, size), :], sems.at[i]
        )
        for i, (first, size, out) in enumerate(
            [(0, depth, near_ref), (0, mid, top_ref), (mid, mid, bottom_ref)]
        )
    ]
    for copy in copies:
        copy.start()
    slot_copy = pltpu.make_async_copy(slot_hbm, slot_ref, sems.at[3])
    slot_copy.start()
    slot_copy.wait()
    note = slot_note(slot_ref, width)
    near_ref[depth:, :] = note
    top_ref[mid:, :] = note
    bottom_ref[mid:, :] = note
    for copy in copies:
        copy.wait()


def slot_note(slot_ref, width):
    row = lax.broadcasted_iota(jnp.int32, (SLOT_ROWS, width), 0)
    note = jnp.zeros((SLOT_ROWS, width), jnp.int32)
    for s in range(slot_ref.shape[0]):
        note = jnp.where(row == s, slot_ref[s], note)
    return note.astype(F32).astype(BF16)


def adapters_kernel(tiles, share_ref, slot_ref, codes_ref, weight_ref, out_ref, scr):
    groups = out_ref.shape[0]
    rows = groups * TPG
    tasks = codes_ref.shape[0]
    row = lax.broadcasted_iota(jnp.int32, (rows, 1), 0)
    group, task = row // TPG, row % TPG
    live = jnp.zeros((rows, 1), jnp.int32)
    for g in range(groups):
        task = task + jnp.where(group > g, share_ref[g], 0)
        live = live + jnp.where(group == g, share_ref[g], 0)
    task = jnp.where(row % TPG < live, task, -1)
    pick = (task == lax.broadcasted_iota(jnp.int32, (rows, tasks), 1)).astype(BF16)
    chosen = dot(pick, codes_ref[...]).astype(BF16)
    for k in range(tiles):
        part = dot(chosen, weight_ref[:, k * LANES : (k + 1) * LANES])
        scr[pl.ds(k, rows, stride=tiles), :] = part
    note = slot_note(slot_ref, LANES)
    for g in range(groups):
        at = g * TPG * tiles
        out_ref[g, : TPG * tiles, :] = scr[at : at + TPG * tiles, :].astype(BF16)
        out_ref[g, TPG * tiles :, :] = note


def choose_kernel(tiles, n, slot_ref, *refs):
    note_refs, got_ref, out_refs = refs[: n - 1], refs[n - 1], refs[n:]
    seqs = slot_ref.shape[0]
    groups = got_ref.shape[0]
    row = lax.broadcasted_iota(jnp.int32, (groups * seqs, LANES), 0)
    table = jnp.zeros((groups * seqs, LANES), F32)
    for g in range(groups):
        notes = got_ref[g, TPG * tiles :, :].astype(F32)
        for s in range(seqs):
            table = jnp.where(row == g * seqs + s, notes[s : s + 1, :], table)
    table = table.astype(BF16)
    for k, out in enumerate(out_refs):
        if k > 0:
            note_ref = note_refs[k - 1]
            notes = note_ref[note_ref.shape[0] - SLOT_ROWS :, :].astype(F32).astype(jnp.int32)
        for s in range(seqs):
            slot = slot_ref[s] if k == 0 else jnp.max(notes[s : s + 1, :])
            rows = pl.ds(pl.multiple_of(slot * tiles, 16), tiles)
            for g in range(groups):
                at = (g * seqs + s) * tiles
                out[at : at + tiles, :] = got_ref[g, rows, :]
        out[groups * seqs * tiles :, :] = table


def low_rank_kernel(
    tiles, place_ref, share_ref, codes_ref, adapt_refs, tokens_ref,
    low_ref, b4_ref, tok_t_ref, codes_t_ref, scr, held, table,
):
    n = len(adapt_refs)
    seqs = b4_ref.shape[0]
    groups = share_ref.shape[0]
    per_part = groups * seqs
    for k, part in enumerate(adapt_refs):
        table[k * per_part : (k + 1) * per_part, :] = part[per_part * tiles :, :].astype(F32)
        for g in range(groups):
            at = pl.multiple_of((g * n + (place_ref[0] ^ k)) * tiles, 16)
            for s in range(seqs):
                first = (g * seqs + s) * tiles
                held[s, pl.ds(at, tiles), :] = part[first : first + tiles, :]
    rows, tasks = table.shape[0], codes_ref.shape[0]
    task = table[:, :1].astype(jnp.int32)
    group = lax.broadcasted_iota(jnp.int32, (rows, 1), 0) % per_part // seqs
    for g in range(groups - 1):
        task = task + jnp.where(group > g, share_ref[g], 0)
    pick = (task == lax.broadcasted_iota(jnp.int32, (rows, tasks), 1)).astype(BF16)
    codes = dot(pick, codes_ref[...]).astype(BF16)
    at = lax.broadcasted_iota(jnp.int32, (rows, rows), 1)
    source = at % per_part // seqs * n + (place_ref[0] ^ (at // per_part))
    order = source * seqs + at % seqs == lax.broadcasted_iota(jnp.int32, (rows, rows), 0)
    codes_t_ref[...] = dot(order.astype(BF16), codes).T.astype(BF16)
    low_rank_body(held, tokens_ref, low_ref, b4_ref, tok_t_ref, scr)


def low_rank_body(adapt_ref, tokens_ref, low_ref, b4_ref, tok_t_ref, scr):
    seqs = b4_ref.shape[0]
    lane = lax.broadcasted_iota(jnp.int32, (BLOCK_D, LANES * seqs), 1)
    row = lax.broadcasted_iota(jnp.int32, (BLOCK_D, LANES * seqs), 0)
    keep = (lane % LANES) // R == row % PACK
    spread = (
        lax.broadcasted_iota(jnp.int32, (BLOCK_D, BLOCK_Q), 0) // PACK
        == lax.broadcasted_iota(jnp.int32, (BLOCK_D, BLOCK_Q), 1)
    ).astype(BF16)
    to = lax.broadcasted_iota(jnp.int32, (BLOCK_D, BLOCK_D), 0)
    sort = (
        to % BLOCK_Q * PACK + to // BLOCK_Q
        == lax.broadcasted_iota(jnp.int32, (BLOCK_D, BLOCK_D), 1)
    ).astype(BF16)
    acc = jnp.zeros((tokens_ref.shape[0], LANES * seqs), F32)
    for b in range(D // BLOCK_D):
        cols = slice(b * BLOCK_D, (b + 1) * BLOCK_D)
        part = jnp.concatenate(
            [adapt_ref[s, b * BLOCK_Q : (b + 1) * BLOCK_Q, :] for s in range(seqs)], axis=1
        )
        wide = jnp.where(keep, dot(spread, part), 0.0).astype(BF16)
        block = tokens_ref[:, cols]
        acc = acc + dot(block, wide)
        turned = dot_nt(sort, block).astype(BF16)
        for j in range(PACK):
            tok_t_ref[
                b * BLOCK_Q : (b + 1) * BLOCK_Q, j * block.shape[0] : (j + 1) * block.shape[0]
            ] = turned[j * BLOCK_Q : (j + 1) * BLOCK_Q, :]
    first = lax.broadcasted_iota(jnp.int32, (SEQ_LEN, LANES), 1) < R
    for s in range(seqs):
        z = acc[s * SEQ_LEN : (s + 1) * SEQ_LEN, s * LANES : (s + 1) * LANES]
        total = z
        for j in range(1, PACK):
            total = total + pltpu.roll(z, j * R, 1)
        low_ref[s * SEQ_LEN : (s + 1) * SEQ_LEN, :] = jnp.where(first, total * SHRINK, 0.0).astype(
            BF16
        )
        scr[...] = adapt_ref[s, A_ROWS:, :].astype(F32)
        for c in range(COL_TILES):
            piece = scr[pl.ds(c, R, stride=COL_TILES), :].astype(BF16)
            for j in range(PACK):
                b4_ref[s, j * R : (j + 1) * R, c * LANES : (c + 1) * LANES] = piece


def frozen_kernel(n_tok, depth, own, layout, has_acc, place_ref, *refs):
    refs = iter(refs)
    token_refs = [next(refs) for _ in range(n_tok)]
    weight_ref = next(refs) if own else None
    sets = [
        ([(m, next(refs)) for m in masks], segments) for masks, segments in layout
    ]
    accs = [next(refs) for _ in range(n_tok)] if has_acc else [None] * n_tok
    outs = list(refs)
    me, core, chip = place_ref[0], place_ref[1], place_ref[2]
    width = sets[0][0][0][1].shape[1]

    def cols(k, first, size):
        return pl.ds(pl.multiple_of((me ^ k) * depth + first, LANES), size)

    for tok, acc, out in zip(token_refs, accs, outs):
        if own:
            half = out.shape[1]
            block = weight_ref[:, pl.ds(pl.multiple_of(core * half, LANES), half)]
            out[...] = dot(tok[:, cols(0, 0, depth)], block)
        else:
            out[...] = acc[...]
        for pieces, segments in sets:
            for first_chip in range(0, len(pieces), 2):
                pair = pieces[first_chip : first_chip + 2]
                part = None
                for k, first, size, row in segments:
                    right = jnp.concatenate([x[row : row + size, :] for _, x in pair], axis=1)
                    term = dot(tok[:, cols(k, first, size)], right)
                    part = term if part is None else part + term
                for at, (mask, _) in enumerate(pair):
                    where = pl.ds(pl.multiple_of((chip ^ mask) * width, LANES), width)
                    out[:, where] += part[:, at * width : (at + 1) * width]


def frozen_layout(sets):
    layout = [([m for m, _ in pieces], segments) for pieces, segments in sets]
    return layout, [x for pieces, _ in sets for _, x in pieces]


def frozen_call(place, depth, half, tokens, weight, sets, accs):
    rows = tokens[0].shape[0]
    layout, flat = frozen_layout(sets)
    size = 2 * rows * sum(x.size for x in flat) + (0 if weight is None else 2 * rows * depth * half)
    weights = [] if weight is None else [weight]
    return call(
        functools.partial(
            frozen_kernel, len(tokens), depth, weight is not None, layout, bool(accs)
        ),
        [sds((rows, half), F32)] * len(tokens),
        n_smem=1,
        n_in=len(tokens) + len(weights) + len(flat) + len(accs),
        flops=size * len(tokens),
        nbytes=2 * sum(x.size for x in flat) + 4 * rows * half * len(tokens),
    )(place, *tokens, *weights, *flat, *accs)


def backward_kernel(
    loss_scale, place_ref, share_ref, slot_ref, counts_ref, mine_ref, theirs_ref, teacher_ref, low_ref, b4_ref, tok_t_ref, out_ref,
    values, spaced, grads,
):
    seqs = b4_ref.shape[0]
    half = mine_ref.shape[1]
    core, group = place_ref[1], place_ref[3]
    n_tasks = counts_ref.shape[0]
    first_task = jnp.int32(0)
    for g in range(share_ref.shape[0]):
        first_task = first_task + jnp.where(g < group, share_ref[g], 0)
    all_counts = counts_ref[0]
    for t in range(1, n_tasks):
        all_counts = all_counts + counts_ref[t]
    values[:, pl.ds(pl.multiple_of(core * half, LANES), half)] = mine_ref[...]
    values[:, pl.ds(pl.multiple_of((1 - core) * half, LANES), half)] = theirs_ref[...]
    blocks = []
    for s in range(seqs):
        rows = slice(s * SEQ_LEN, (s + 1) * SEQ_LEN)
        low = low_ref[rows, :]
        b4 = b4_ref[s]
        error = values[rows, :] + dot(low, b4) * RANK_SCALE - teacher_ref[rows, :].astype(F32)
        count = jnp.full((1, KV), counts_ref[first_task + slot_ref[s]], jnp.int32).astype(F32)
        mean = jnp.full((1, KV), all_counts, jnp.int32).astype(F32) / n_tasks
        value_grad = (error * (mean / count * loss_scale)).astype(BF16)
        blocks.append((dot_nt(value_grad, b4) * RANK_SCALE).astype(BF16))
        second = dot(low.T, value_grad)[:R] * RANK_SCALE
        for c in range(COL_TILES):
            spaced[pl.ds(c, R, stride=COL_TILES), :] = second[:, c * LANES : (c + 1) * LANES]
        grads[s, A_ROWS:, :] = spaced[...].astype(BF16)
    zero = jnp.zeros_like(blocks[0])
    low_grad = jnp.concatenate(
        [
            jnp.concatenate([blocks[s] if s == i else zero for i in range(seqs)], axis=1)
            for s in range(seqs)
        ],
        axis=0,
    )
    group = lax.broadcasted_iota(jnp.int32, low_grad.shape, 1) % LANES // R
    low_grad = jnp.concatenate(
        [jnp.where(group == j, low_grad, jnp.zeros_like(low_grad)) for j in range(PACK)], axis=0
    )
    first = (dot(tok_t_ref[...], low_grad) * SHRINK).astype(BF16)
    for s in range(seqs):
        grads[s, :A_ROWS, :] = first[:, s * LANES : (s + 1) * LANES]
    store_grads(grads, out_ref)


def store_grads(grads, out_ref):
    if len(out_ref.shape) == 3:
        out_ref[...] = grads[...]
        return
    tiles = out_ref.shape[2]
    for i in range(out_ref.shape[0]):
        for s in range(out_ref.shape[1]):
            out_ref[i, s] = grads[s, i * tiles : (i + 1) * tiles, :]


def hyper_kernel(step, codes_t_ref, grads_ref, out_ref, scr, done, sems):
    devices, seqs, tiles, _ = grads_ref.shape
    rows = devices * seqs
    for i in range(devices):
        for s in range(seqs):
            at = (i * seqs + s) * tiles
            scr[at : at + tiles, :] = grads_ref[i, s].astype(F32)
    codes_t = codes_t_ref[...]
    copies = []
    for k in range(tiles):
        part = scr[pl.ds(k, rows, stride=tiles), :].astype(BF16)
        done[:, k * LANES : (k + 1) * LANES] = dot(codes_t, part)
        if (k + 1) % step == 0:
            cols = slice((k + 1 - step) * LANES, (k + 1) * LANES)
            copies.append(
                pltpu.make_async_copy(done.at[:, cols], out_ref.at[:, cols], sems.at[k // step])
            )
            copies[-1].start()
    for copy in copies:
        copy.wait()


def tied(*groups):
    return lax.optimization_barrier(groups)


def shards(
    task_codes, hyper_weight, frozen_weight, tokens, teacher, seq_slot, task_share, token_counts
):
    groups = lax.axis_size("dp")
    members = lax.axis_size("mp")
    devices = groups * members
    chips = groups // 2
    tok_dev = tokens.shape[0]
    seqs = seq_slot.shape[0]
    depth = frozen_weight.shape[0]
    tiles = hyper_weight.shape[1] // LANES
    rows = A_ROWS + B_ROWS
    width_h = task_codes.shape[1]
    loss_scale = 1.0 / math.sqrt(tok_dev * members)
    me_dp, me_mp = lax.axis_index("dp"), lax.axis_index("mp")
    core, chip = me_dp % 2, me_dp // 2
    place = jnp.stack([me_mp, core, chip, me_dp]).astype(jnp.int32)
    half = KV // 2
    width = half // chips
    whole_tiles = tiles % 16 == 0

    mid = depth // 2

    def direct(block):
        return {
            m: xor_permute(block, "dp", m << 1) if m else block
            for m in range(chips)
            if m & (m - 1) == 0
        }

    def forwarded(held, by_high):
        held = dict(held)
        for m in range(1, chips):
            if m not in held:
                bit = 1 << (m.bit_length() - 1) if by_high else m & -m
                held[m] = xor_permute(held[m ^ bit], "dp", bit << 1)
        return held

    other_tokens = xor_permute(tokens, "dp", 1)
    fits = width % LANES == 0 and mid % LANES == 0 and members == 4 and chips == 4
    fits = fits and whole_tiles and groups * seqs % 16 == 0
    near_rows = [(1, 0, depth, 0)]
    if fits:
        near, top, bottom = pl.pallas_call(
            chunk_kernel,
            in_specs=[pl.BlockSpec(memory_space=pltpu.SMEM)]
            + [pl.BlockSpec(memory_space=pltpu.HBM)] * 2,
            out_specs=[pl.BlockSpec(memory_space=pltpu.VMEM)] * 3,
            out_shape=[sds((n + SLOT_ROWS, width), BF16) for n in (depth, mid, mid)],
            scratch_shapes=[
                pltpu.SMEM(seq_slot.shape, jnp.int32),
                pltpu.SemaphoreType.DMA((4,)),
            ],
            compiler_params=pltpu.CompilerParams(vmem_limit_bytes=ALL_VMEM),
        )(place, seq_slot, frozen_weight)
        near, top, bottom, task_codes = tied(near, top, bottom, task_codes)
        other_tokens, task_codes = tied(other_tokens, task_codes)
        near = xor_permute(near, "mp", 1)
        top = xor_permute(top, "mp", 2)
        bottom = xor_permute(bottom, "mp", 3)
        near_held = direct(near)
        far = jnp.concatenate([top, bottom], axis=0)
        at = mid + SLOT_ROWS
        far_rows = [(2, 0, mid, 0), (3, mid, mid, at)]
        third_rows = [(3, 0, mid, 0), (2, mid, mid, at)]
        note_parts = [near, top, bottom]
    else:
        chunk = lax.dynamic_slice_in_dim(frozen_weight, core * half + chip * width, width, 1)
        near = xor_permute(chunk, "mp", 1)
        near_held = direct(near)
        far = jnp.concatenate(
            [xor_permute(chunk, "mp", k) for k in range(2, members)], axis=0
        )
        far_rows = [(k, 0, depth, (k - 2) * depth) for k in range(2, members)]

    if fits:
        sent = call(
            functools.partial(adapters_kernel, tiles),
            [sds((groups, TPG * tiles + SLOT_ROWS, LANES), BF16)],
            scratch=[pltpu.VMEM((groups * TPG * tiles, LANES), F32)],
            n_smem=2,
            n_in=2,
            flops=2 * groups * TPG * hyper_weight.size,
            nbytes=4 * hyper_weight.size,
        )(task_share, seq_slot, task_codes, hyper_weight)[0]
        got = lax.all_to_all(sent, "dp", 0, 0, tiled=True)
        chosen = call(
            functools.partial(choose_kernel, tiles, members),
            [sds((groups * seqs * (tiles + 1), LANES), BF16)] * members,
            n_smem=1,
            n_in=members,
            nbytes=8 * hyper_weight.size,
        )(seq_slot, *note_parts, got)
        near_held, far, chosen = tied(near_held, far, chosen)
        third = xor_permute(far, "mp", 1)
        near_pieces = forwarded(near_held, True)
        adapt = [chosen[0]] + [xor_permute(chosen[k], "mp", k) for k in range(1, members)]
    else:
        near_pieces = forwarded(near_held, True)
        slots = lax.all_to_all(
            jnp.broadcast_to(seq_slot[None], (devices, seqs)), ("dp", "mp"), 0, 0, tiled=True
        ).reshape(-1)
        offsets = jnp.cumsum(task_share) - task_share
        task_of = jnp.repeat(offsets, members * seqs) + slots
        pick = (jnp.arange(task_codes.shape[0])[:, None] == task_of[None, :]).astype(BF16)
        codes_t = dot(task_codes.T, pick).astype(BF16)
        sent = dot(codes_t.T, hyper_weight).astype(BF16).reshape(devices, seqs, tiles, LANES)
        adapt = lax.all_to_all(sent, ("dp", "mp"), 0, 0, tiled=True)
        adapt = adapt.transpose(1, 0, 2, 3).reshape(seqs, rows, LANES)

    far_held = direct(far)
    if fits:
        third_held = direct(third)
        sets = [(list(near_pieces.items()), near_rows)]
        accs = frozen_call(place, depth, half, [tokens, other_tokens], frozen_weight, sets, [])
        third_held, far_held, accs, adapt = tied(third_held, far_held, accs, adapt)
        third_pieces = forwarded(third_held, True)
    far_pieces = forwarded(far_held, False)

    low_outs = [
        sds((tok_dev, LANES), BF16),
        sds((seqs, LANES, KV), BF16),
        sds((D // PACK, PACK * tok_dev), BF16),
    ]
    low_cost = dict(
        flops=4 * tokens.size * LANES * seqs, nbytes=4 * tokens.size + 4 * seqs * rows * LANES
    )
    low_scratch = [pltpu.VMEM((B_ROWS, LANES), F32)]
    if fits:
        last = chips - 1
        sets = [
            ([(m, far_held[m]) for m in far_held], far_rows),
            ([(m, third_held[m]) for m in third_held], third_rows),
        ]
        layout, flat = frozen_layout(sets)
        n_flat, n_adapt = len(flat), len(adapt)

        def middle(*refs):
            refs = list(refs)
            place_ref, share_ref, codes_ref = refs[:3]
            token_refs, refs = refs[3:5], refs[5:]
            piece_refs, refs = refs[:n_flat], refs[n_flat:]
            acc_refs, refs = refs[:2], refs[2:]
            adapt_refs, refs = refs[:n_adapt], refs[n_adapt:]
            out_refs, refs = refs[:2], refs[2:]
            low_rank_kernel(
                tiles, place_ref, share_ref, codes_ref, adapt_refs, token_refs[0], *refs
            )
            frozen_kernel(
                2, depth, False, layout, True, place_ref, *token_refs, *piece_refs, *acc_refs,
                *out_refs,
            )

        *accs, low, b4, tok_t, codes_t = call(
            middle,
            [sds((tok_dev, half), F32)] * 2
            + low_outs
            + [sds((width_h, devices * seqs), BF16)],
            scratch=low_scratch
            + [
                pltpu.VMEM((seqs, rows, LANES), BF16),
                pltpu.VMEM((devices * seqs, LANES), F32),
            ],
            n_smem=2,
            n_in=5 + n_flat + n_adapt,
        )(place, task_share, task_codes, tokens, other_tokens, *flat, *accs, *adapt)
        sets = [([(last, far_pieces[last])], far_rows), ([(last, third_pieces[last])], third_rows)]
        theirs = frozen_call(place, depth, half, [other_tokens], None, sets, accs[1:])[0]
        mine = frozen_call(place, depth, half, [tokens], None, sets, accs[:1])[0]
    else:
        low, b4, tok_t = call(
            low_rank_body, low_outs, scratch=low_scratch, n_in=2, **low_cost
        )(adapt, tokens)
        own_half = lax.dynamic_slice_in_dim(frozen_weight, core * half, half, 1)
        order = jnp.arange(chips) ^ chip
        found = {0: own_half}
        for pieces, segments in ((near_pieces, near_rows), (far_pieces, far_rows)):
            joined = jnp.stack([pieces[m] for m in range(chips)])
            joined = jnp.take(joined, order, axis=0).transpose(1, 0, 2).reshape(-1, half)
            for k, _, size, row in segments:
                found[k] = joined[row : row + size]
        blocks = jnp.stack([found[k] for k in range(members)])
        weight = jnp.take(blocks, jnp.arange(members) ^ me_mp, axis=0).reshape(D, half)
        mine = jnp.dot(tokens, weight, preferred_element_type=F32)
        theirs = jnp.dot(other_tokens, weight, preferred_element_type=F32)
    received = xor_permute(theirs, "dp", 1)

    split = (devices, seqs, tiles, LANES)
    grads = call(
        functools.partial(backward_kernel, loss_scale),
        [sds(split if whole_tiles else (seqs, rows, LANES), BF16)],
        scratch=[
            pltpu.VMEM((tok_dev, KV), F32),
            pltpu.VMEM((B_ROWS, LANES), F32),
            pltpu.VMEM((seqs, rows, LANES), BF16),
        ],
        n_smem=4,
        n_in=6,
        flops=4 * tokens.size * LANES * seqs,
        nbytes=4 * tokens.size,
    )(place, task_share, seq_slot, token_counts, mine, received, teacher, low, b4, tok_t)[0]
    if not whole_tiles:
        grads = grads.reshape(seqs, devices, tiles, LANES).transpose(1, 0, 2, 3)
    routed = lax.all_to_all(grads, ("dp", "mp"), 0, 0, tiled=True)
    step = 8 if whole_tiles else tiles
    return pl.pallas_call(
        functools.partial(hyper_kernel, step),
        out_shape=sds((width_h, tiles * LANES), F32),
        in_specs=[pl.BlockSpec(memory_space=pltpu.VMEM)] * 2,
        out_specs=pl.BlockSpec(memory_space=pl.ANY),
        scratch_shapes=[
            pltpu.VMEM((devices * seqs * tiles, LANES), F32),
            pltpu.VMEM((width_h, tiles * LANES), F32),
            pltpu.SemaphoreType.DMA((tiles // step,)),
        ],
        compiler_params=pltpu.CompilerParams(vmem_limit_bytes=VMEM_LIMIT),
    )(codes_t, routed)


def solution(mesh):
    placed = (
        P(),
        P(None, ("dp", "mp")),
        P("mp", None),
        P(("dp", "mp"), None),
        P(("dp", "mp"), None),
        P(("dp", "mp")),
        P(),
        P(),
    )
    return jax.shard_map(
        shards, mesh=mesh, in_specs=placed, out_specs=P(None, ("dp", "mp")), check_vma=False
    )
```

```python
import functools
import math

import jax
import jax.numpy as jnp
from jax import lax
from jax.experimental import pallas as pl
from jax.experimental.pallas import tpu as pltpu
from jax.sharding import PartitionSpec as P

D = 5120
KV = 1024
R = 32
TPG = 4
SEQ_LEN = 128
LANES = 128
PACK = LANES // R
SLOT_ROWS = 16
A_ROWS = D * R // LANES
B_ROWS = R * KV // LANES
COL_TILES = KV // LANES
BLOCK_D = 512
BLOCK_Q = BLOCK_D // PACK
SHRINK = 1.0 / math.sqrt(D)
RANK_SCALE = 1.0 / math.sqrt(R)
F32 = jnp.float32
BF16 = jnp.bfloat16
VMEM_LIMIT = 16 * 1024 * 1024
ALL_VMEM = 56 * 1024 * 1024


def dot(a, b):
    return jnp.dot(a, b, preferred_element_type=F32)


def dot_nt(a, b):
    return lax.dot_general(a, b, (((1,), (1,)), ((), ())), preferred_element_type=F32)


def call(body, outs, scratch=(), n_smem=0, n_in=0, flops=0, nbytes=0, **kw):
    specs = [pl.BlockSpec(memory_space=pltpu.SMEM)] * n_smem
    specs += [pl.BlockSpec(memory_space=pltpu.VMEM)] * n_in
    out_specs = [pl.BlockSpec(memory_space=pltpu.VMEM)] * len(outs)
    return pl.pallas_call(
        body,
        out_shape=list(outs),
        in_specs=specs,
        out_specs=out_specs,
        scratch_shapes=list(scratch),
        compiler_params=pltpu.CompilerParams(vmem_limit_bytes=VMEM_LIMIT),
        cost_estimate=pl.CostEstimate(flops=flops, bytes_accessed=nbytes, transcendentals=0),
        **kw,
    )


def sds(shape, dtype):
    return jax.ShapeDtypeStruct(shape, dtype)


def xor_permute(array, axis, mask):
    return lax.ppermute(array, axis, [(i, i ^ mask) for i in range(lax.axis_size(axis))])


def chunk_kernel(place_ref, slot_hbm, weight_ref, near_ref, top_ref, bottom_ref, slot_ref, sems):
    depth = weight_ref.shape[0]
    width = near_ref.shape[1]
    mid = depth // 2
    half = weight_ref.shape[1] // 2
    at = pl.ds(pl.multiple_of(place_ref[1] * half + place_ref[2] * width, LANES), width)
    copies = [
        pltpu.make_async_copy(
            weight_ref.at[pl.ds(first, size), at], out.at[pl.ds(0, size), :], sems.at[i]
        )
        for i, (first, size, out) in enumerate(
            [(0, depth, near_ref), (0, mid, top_ref), (mid, mid, bottom_ref)]
        )
    ]
    for copy in copies:
        copy.start()
    slot_copy = pltpu.make_async_copy(slot_hbm, slot_ref, sems.at[3])
    slot_copy.start()
    slot_copy.wait()
    note = slot_note(slot_ref, width)
    near_ref[depth:, :] = note
    top_ref[mid:, :] = note
    bottom_ref[mid:, :] = note
    for copy in copies:
        copy.wait()


def slot_note(slot_ref, width):
    row = lax.broadcasted_iota(jnp.int32, (SLOT_ROWS, width), 0)
    note = jnp.zeros((SLOT_ROWS, width), jnp.int32)
    for s in range(slot_ref.shape[0]):
        note = jnp.where(row == s, slot_ref[s], note)
    return note.astype(F32).astype(BF16)


def adapters_kernel(tiles, share_ref, slot_ref, codes_ref, weight_ref, out_ref, scr):
    groups = out_ref.shape[0]
    rows = groups * TPG
    tasks = codes_ref.shape[0]
    row = lax.broadcasted_iota(jnp.int32, (rows, 1), 0)
    group, task = row // TPG, row % TPG
    live = jnp.zeros((rows, 1), jnp.int32)
    for g in range(groups):
        task = task + jnp.where(group > g, share_ref[g], 0)
        live = live + jnp.where(group == g, share_ref[g], 0)
    task = jnp.where(row % TPG < live, task, -1)
    pick = (task == lax.broadcasted_iota(jnp.int32, (rows, tasks), 1)).astype(BF16)
    chosen = dot(pick, codes_ref[...]).astype(BF16)
    for k in range(tiles):
        part = dot(chosen, weight_ref[:, k * LANES : (k + 1) * LANES])
        scr[pl.ds(k, rows, stride=tiles), :] = part
    note = slot_note(slot_ref, LANES)
    for g in range(groups):
        at = g * TPG * tiles
        out_ref[g, : TPG * tiles, :] = scr[at : at + TPG * tiles, :].astype(BF16)
        out_ref[g, TPG * tiles :, :] = note


def choose_kernel(tiles, slot_ref, near_ref, far_ref, got_ref, *out_refs):
    seqs = slot_ref.shape[0]
    groups = got_ref.shape[0]
    row = lax.broadcasted_iota(jnp.int32, (groups * seqs, LANES), 0)
    table = jnp.zeros((groups * seqs, LANES), F32)
    for g in range(groups):
        notes = got_ref[g, TPG * tiles :, :].astype(F32)
        for s in range(seqs):
            table = jnp.where(row == g * seqs + s, notes[s : s + 1, :], table)
    table = table.astype(BF16)
    far_rows = far_ref.shape[0]
    out_refs[1][:far_rows, :] = far_ref[...]
    note_ends = [None, (near_ref, near_ref.shape[0]), (far_ref, far_rows // 2), (far_ref, far_rows)]
    for k, out in enumerate(out_refs):
        if k > 0:
            note_ref, end = note_ends[k]
            notes = note_ref[end - SLOT_ROWS : end, :].astype(F32).astype(jnp.int32)
        if k == 1:
            out = out.at[far_rows:, :]
        for s in range(seqs):
            slot = slot_ref[s] if k == 0 else jnp.max(notes[s : s + 1, :])
            rows = pl.ds(pl.multiple_of(slot * tiles, 16), tiles)
            for g in range(groups):
                at = (g * seqs + s) * tiles
                out[at : at + tiles, :] = got_ref[g, rows, :]
        out[groups * seqs * tiles :, :] = table


def low_rank_kernel(
    tiles, place_ref, share_ref, codes_ref, adapt_refs, tokens_ref,
    low_ref, b4_ref, tok_t_ref, codes_t_ref, scr, held, table,
):
    n = len(adapt_refs)
    seqs = b4_ref.shape[0]
    groups = share_ref.shape[0]
    per_part = groups * seqs
    for k, part in enumerate(adapt_refs):
        part = part.at[part.shape[0] - per_part * (tiles + 1) :, :]
        table[k * per_part : (k + 1) * per_part, :] = part[per_part * tiles :, :].astype(F32)
        for g in range(groups):
            at = pl.multiple_of((g * n + (place_ref[0] ^ k)) * tiles, 16)
            for s in range(seqs):
                first = (g * seqs + s) * tiles
                held[s, pl.ds(at, tiles), :] = part[first : first + tiles, :]
    rows, tasks = table.shape[0], codes_ref.shape[0]
    task = table[:, :1].astype(jnp.int32)
    group = lax.broadcasted_iota(jnp.int32, (rows, 1), 0) % per_part // seqs
    for g in range(groups - 1):
        task = task + jnp.where(group > g, share_ref[g], 0)
    pick = (task == lax.broadcasted_iota(jnp.int32, (rows, tasks), 1)).astype(BF16)
    codes = dot(pick, codes_ref[...]).astype(BF16)
    at = lax.broadcasted_iota(jnp.int32, (rows, rows), 1)
    source = at % per_part // seqs * n + (place_ref[0] ^ (at // per_part))
    order = source * seqs + at % seqs == lax.broadcasted_iota(jnp.int32, (rows, rows), 0)
    codes_t_ref[...] = dot(order.astype(BF16), codes).T.astype(BF16)
    low_rank_body(held, tokens_ref, low_ref, b4_ref, tok_t_ref, scr)


def low_rank_body(adapt_ref, tokens_ref, low_ref, b4_ref, tok_t_ref, scr):
    seqs = b4_ref.shape[0]
    lane = lax.broadcasted_iota(jnp.int32, (BLOCK_D, LANES * seqs), 1)
    row = lax.broadcasted_iota(jnp.int32, (BLOCK_D, LANES * seqs), 0)
    keep = (lane % LANES) // R == row % PACK
    spread = (
        lax.broadcasted_iota(jnp.int32, (BLOCK_D, BLOCK_Q), 0) // PACK
        == lax.broadcasted_iota(jnp.int32, (BLOCK_D, BLOCK_Q), 1)
    ).astype(BF16)
    to = lax.broadcasted_iota(jnp.int32, (BLOCK_D, BLOCK_D), 0)
    sort = (
        to % BLOCK_Q * PACK + to // BLOCK_Q
        == lax.broadcasted_iota(jnp.int32, (BLOCK_D, BLOCK_D), 1)
    ).astype(BF16)
    acc = jnp.zeros((tokens_ref.shape[0], LANES * seqs), F32)
    for b in range(D // BLOCK_D):
        cols = slice(b * BLOCK_D, (b + 1) * BLOCK_D)
        part = jnp.concatenate(
            [adapt_ref[s, b * BLOCK_Q : (b + 1) * BLOCK_Q, :] for s in range(seqs)], axis=1
        )
        wide = jnp.where(keep, dot(spread, part), 0.0).astype(BF16)
        block = tokens_ref[:, cols]
        acc = acc + dot(block, wide)
        turned = dot_nt(sort, block).astype(BF16)
        for j in range(PACK):
            tok_t_ref[
                b * BLOCK_Q : (b + 1) * BLOCK_Q, j * block.shape[0] : (j + 1) * block.shape[0]
            ] = turned[j * BLOCK_Q : (j + 1) * BLOCK_Q, :]
    first = lax.broadcasted_iota(jnp.int32, (SEQ_LEN, LANES), 1) < R
    for s in range(seqs):
        z = acc[s * SEQ_LEN : (s + 1) * SEQ_LEN, s * LANES : (s + 1) * LANES]
        total = z
        for j in range(1, PACK):
            total = total + pltpu.roll(z, j * R, 1)
        low_ref[s * SEQ_LEN : (s + 1) * SEQ_LEN, :] = jnp.where(first, total * SHRINK, 0.0).astype(
            BF16
        )
        scr[...] = adapt_ref[s, A_ROWS:, :].astype(F32)
        for c in range(COL_TILES):
            piece = scr[pl.ds(c, R, stride=COL_TILES), :].astype(BF16)
            for j in range(PACK):
                b4_ref[s, j * R : (j + 1) * R, c * LANES : (c + 1) * LANES] = piece


def frozen_kernel(n_tok, depth, own, layout, has_acc, place_ref, *refs):
    refs = iter(refs)
    token_refs = [next(refs) for _ in range(n_tok)]
    weight_ref = next(refs) if own else None
    sets = [
        ([(m, next(refs)) for m in masks], segments) for masks, segments in layout
    ]
    accs = [next(refs) for _ in range(n_tok)] if has_acc else [None] * n_tok
    outs = list(refs)
    me, core, chip = place_ref[0], place_ref[1], place_ref[2]
    width = sets[0][0][0][1].shape[1]

    def cols(k, first, size):
        return pl.ds(pl.multiple_of((me ^ k) * depth + first, LANES), size)

    for tok, acc, out in zip(token_refs, accs, outs):
        if own:
            half = out.shape[1]
            block = weight_ref[:, pl.ds(pl.multiple_of(core * half, LANES), half)]
            out[...] = dot(tok[:, cols(0, 0, depth)], block)
        else:
            out[...] = acc[...]
        for pieces, segments in sets:
            for first_chip in range(0, len(pieces), 2):
                pair = pieces[first_chip : first_chip + 2]
                part = None
                for k, first, size, row in segments:
                    right = jnp.concatenate([x[row : row + size, :] for _, x in pair], axis=1)
                    term = dot(tok[:, cols(k, first, size)], right)
                    part = term if part is None else part + term
                for at, (mask, _) in enumerate(pair):
                    where = pl.ds(pl.multiple_of((chip ^ mask) * width, LANES), width)
                    out[:, where] += part[:, at * width : (at + 1) * width]


def frozen_layout(sets):
    layout = [([m for m, _ in pieces], segments) for pieces, segments in sets]
    return layout, [x for pieces, _ in sets for _, x in pieces]


def frozen_call(place, depth, half, tokens, weight, sets, accs):
    rows = tokens[0].shape[0]
    layout, flat = frozen_layout(sets)
    size = 2 * rows * sum(x.size for x in flat) + (0 if weight is None else 2 * rows * depth * half)
    weights = [] if weight is None else [weight]
    return call(
        functools.partial(
            frozen_kernel, len(tokens), depth, weight is not None, layout, bool(accs)
        ),
        [sds((rows, half), F32)] * len(tokens),
        n_smem=1,
        n_in=len(tokens) + len(weights) + len(flat) + len(accs),
        flops=size * len(tokens),
        nbytes=2 * sum(x.size for x in flat) + 4 * rows * half * len(tokens),
    )(place, *tokens, *weights, *flat, *accs)


def backward_kernel(
    loss_scale, place_ref, share_ref, slot_ref, counts_ref, mine_ref, theirs_ref, teacher_ref, low_ref, b4_ref, tok_t_ref, out_ref,
    values, spaced, grads,
):
    seqs = b4_ref.shape[0]
    half = mine_ref.shape[1]
    core, group = place_ref[1], place_ref[3]
    n_tasks = counts_ref.shape[0]
    first_task = jnp.int32(0)
    for g in range(share_ref.shape[0]):
        first_task = first_task + jnp.where(g < group, share_ref[g], 0)
    all_counts = counts_ref[0]
    for t in range(1, n_tasks):
        all_counts = all_counts + counts_ref[t]
    values[:, pl.ds(pl.multiple_of(core * half, LANES), half)] = mine_ref[...]
    values[:, pl.ds(pl.multiple_of((1 - core) * half, LANES), half)] = theirs_ref[...]
    blocks = []
    for s in range(seqs):
        rows = slice(s * SEQ_LEN, (s + 1) * SEQ_LEN)
        low = low_ref[rows, :]
        b4 = b4_ref[s]
        error = values[rows, :] + dot(low, b4) * RANK_SCALE - teacher_ref[rows, :].astype(F32)
        count = jnp.full((1, KV), counts_ref[first_task + slot_ref[s]], jnp.int32).astype(F32)
        mean = jnp.full((1, KV), all_counts, jnp.int32).astype(F32) / n_tasks
        value_grad = (error * (mean / count * loss_scale)).astype(BF16)
        blocks.append((dot_nt(value_grad, b4) * RANK_SCALE).astype(BF16))
        second = dot(low.T, value_grad)[:R] * RANK_SCALE
        for c in range(COL_TILES):
            spaced[pl.ds(c, R, stride=COL_TILES), :] = second[:, c * LANES : (c + 1) * LANES]
        grads[s, A_ROWS:, :] = spaced[...].astype(BF16)
    zero = jnp.zeros_like(blocks[0])
    low_grad = jnp.concatenate(
        [
            jnp.concatenate([blocks[s] if s == i else zero for i in range(seqs)], axis=1)
            for s in range(seqs)
        ],
        axis=0,
    )
    group = lax.broadcasted_iota(jnp.int32, low_grad.shape, 1) % LANES // R
    low_grad = jnp.concatenate(
        [jnp.where(group == j, low_grad, jnp.zeros_like(low_grad)) for j in range(PACK)], axis=0
    )
    first = (dot(tok_t_ref[...], low_grad) * SHRINK).astype(BF16)
    for s in range(seqs):
        grads[s, :A_ROWS, :] = first[:, s * LANES : (s + 1) * LANES]
    store_grads(grads, out_ref)


def store_grads(grads, out_ref):
    if len(out_ref.shape) == 3:
        out_ref[...] = grads[...]
        return
    tiles = out_ref.shape[2]
    for i in range(out_ref.shape[0]):
        for s in range(out_ref.shape[1]):
            out_ref[i, s] = grads[s, i * tiles : (i + 1) * tiles, :]


def hyper_kernel(step, codes_t_ref, grads_ref, out_ref, scr, done, sems):
    devices, seqs, tiles, _ = grads_ref.shape
    rows = devices * seqs
    for i in range(devices):
        for s in range(seqs):
            at = (i * seqs + s) * tiles
            scr[at : at + tiles, :] = grads_ref[i, s].astype(F32)
    codes_t = codes_t_ref[...]
    copies = []
    for k in range(tiles):
        part = scr[pl.ds(k, rows, stride=tiles), :].astype(BF16)
        done[:, k * LANES : (k + 1) * LANES] = dot(codes_t, part)
        if (k + 1) % step == 0:
            cols = slice((k + 1 - step) * LANES, (k + 1) * LANES)
            copies.append(
                pltpu.make_async_copy(done.at[:, cols], out_ref.at[:, cols], sems.at[k // step])
            )
            copies[-1].start()
    for copy in copies:
        copy.wait()


def tied(*groups):
    return lax.optimization_barrier(groups)


def shards(
    task_codes, hyper_weight, frozen_weight, tokens, teacher, seq_slot, task_share, token_counts
):
    groups = lax.axis_size("dp")
    members = lax.axis_size("mp")
    devices = groups * members
    chips = groups // 2
    tok_dev = tokens.shape[0]
    seqs = seq_slot.shape[0]
    depth = frozen_weight.shape[0]
    tiles = hyper_weight.shape[1] // LANES
    rows = A_ROWS + B_ROWS
    width_h = task_codes.shape[1]
    loss_scale = 1.0 / math.sqrt(tok_dev * members)
    me_dp, me_mp = lax.axis_index("dp"), lax.axis_index("mp")
    core, chip = me_dp % 2, me_dp // 2
    place = jnp.stack([me_mp, core, chip, me_dp]).astype(jnp.int32)
    half = KV // 2
    width = half // chips
    whole_tiles = tiles % 16 == 0

    mid = depth // 2

    def direct(block):
        return {
            m: xor_permute(block, "dp", m << 1) if m else block
            for m in range(chips)
            if m & (m - 1) == 0
        }

    def forwarded(held, by_high):
        held = dict(held)
        for m in range(1, chips):
            if m not in held:
                bit = 1 << (m.bit_length() - 1) if by_high else m & -m
                held[m] = xor_permute(held[m ^ bit], "dp", bit << 1)
        return held

    other_tokens = xor_permute(tokens, "dp", 1)
    fits = width % LANES == 0 and mid % LANES == 0 and members == 4 and chips == 4
    fits = fits and whole_tiles and groups * seqs % 16 == 0
    near_rows = [(1, 0, depth, 0)]
    if fits:
        near, top, bottom = pl.pallas_call(
            chunk_kernel,
            in_specs=[pl.BlockSpec(memory_space=pltpu.SMEM)]
            + [pl.BlockSpec(memory_space=pltpu.HBM)] * 2,
            out_specs=[pl.BlockSpec(memory_space=pltpu.VMEM)] * 3,
            out_shape=[sds((n + SLOT_ROWS, width), BF16) for n in (depth, mid, mid)],
            scratch_shapes=[
                pltpu.SMEM(seq_slot.shape, jnp.int32),
                pltpu.SemaphoreType.DMA((4,)),
            ],
            compiler_params=pltpu.CompilerParams(vmem_limit_bytes=ALL_VMEM),
        )(place, seq_slot, frozen_weight)
        near, top, bottom, task_codes = tied(near, top, bottom, task_codes)
        other_tokens, task_codes = tied(other_tokens, task_codes)
        near = xor_permute(near, "mp", 1)
        top = xor_permute(top, "mp", 2)
        bottom = xor_permute(bottom, "mp", 3)
        near_held = direct(near)
        far = jnp.concatenate([top, bottom], axis=0)
        at = mid + SLOT_ROWS
        far_rows = [(2, 0, mid, 0), (3, mid, mid, at)]
        third_rows = [(3, 0, mid, 0), (2, mid, mid, at)]
    else:
        chunk = lax.dynamic_slice_in_dim(frozen_weight, core * half + chip * width, width, 1)
        near = xor_permute(chunk, "mp", 1)
        near_held = direct(near)
        far = jnp.concatenate(
            [xor_permute(chunk, "mp", k) for k in range(2, members)], axis=0
        )
        far_rows = [(k, 0, depth, (k - 2) * depth) for k in range(2, members)]

    if fits:
        sent = call(
            functools.partial(adapters_kernel, tiles),
            [sds((groups, TPG * tiles + SLOT_ROWS, LANES), BF16)],
            scratch=[pltpu.VMEM((groups * TPG * tiles, LANES), F32)],
            n_smem=2,
            n_in=2,
            flops=2 * groups * TPG * hyper_weight.size,
            nbytes=4 * hyper_weight.size,
        )(task_share, seq_slot, task_codes, hyper_weight)[0]
        got = lax.all_to_all(sent, "dp", 0, 0, tiled=True)
        chosen = call(
            functools.partial(choose_kernel, tiles),
            [
                sds((groups * seqs * (tiles + 1) + (far.shape[0] if k == 1 else 0), LANES), BF16)
                for k in range(members)
            ],
            n_smem=1,
            n_in=3,
            nbytes=8 * hyper_weight.size,
        )(seq_slot, near, far, got)
        near_held, far, chosen = tied(near_held, far, chosen)
        near_pieces = forwarded(near_held, True)
        adapt = [chosen[0]] + [xor_permute(chosen[k], "mp", k) for k in range(1, members)]
        third = adapt[1][: far.shape[0]]
    else:
        near_pieces = forwarded(near_held, True)
        slots = lax.all_to_all(
            jnp.broadcast_to(seq_slot[None], (devices, seqs)), ("dp", "mp"), 0, 0, tiled=True
        ).reshape(-1)
        offsets = jnp.cumsum(task_share) - task_share
        task_of = jnp.repeat(offsets, members * seqs) + slots
        pick = (jnp.arange(task_codes.shape[0])[:, None] == task_of[None, :]).astype(BF16)
        codes_t = dot(task_codes.T, pick).astype(BF16)
        sent = dot(codes_t.T, hyper_weight).astype(BF16).reshape(devices, seqs, tiles, LANES)
        adapt = lax.all_to_all(sent, ("dp", "mp"), 0, 0, tiled=True)
        adapt = adapt.transpose(1, 0, 2, 3).reshape(seqs, rows, LANES)

    far_held = direct(far)
    if fits:
        third_held = direct(third)
        sets = [(list(near_pieces.items()), near_rows)]
        accs = frozen_call(place, depth, half, [tokens, other_tokens], frozen_weight, sets, [])
        third_held, far_held, accs, adapt = tied(third_held, far_held, accs, adapt)
        third_pieces = forwarded(third_held, True)
    far_pieces = forwarded(far_held, False)

    low_outs = [
        sds((tok_dev, LANES), BF16),
        sds((seqs, LANES, KV), BF16),
        sds((D // PACK, PACK * tok_dev), BF16),
    ]
    low_cost = dict(
        flops=4 * tokens.size * LANES * seqs, nbytes=4 * tokens.size + 4 * seqs * rows * LANES
    )
    low_scratch = [pltpu.VMEM((B_ROWS, LANES), F32)]
    if fits:
        last = chips - 1
        sets = [
            ([(m, far_held[m]) for m in far_held], far_rows),
            ([(m, third_held[m]) for m in third_held], third_rows),
        ]
        layout, flat = frozen_layout(sets)
        n_flat, n_adapt = len(flat), len(adapt)

        def middle(*refs):
            refs = list(refs)
            place_ref, share_ref, codes_ref = refs[:3]
            token_refs, refs = refs[3:5], refs[5:]
            piece_refs, refs = refs[:n_flat], refs[n_flat:]
            acc_refs, refs = refs[:2], refs[2:]
            adapt_refs, refs = refs[:n_adapt], refs[n_adapt:]
            out_refs, refs = refs[:2], refs[2:]
            low_rank_kernel(
                tiles, place_ref, share_ref, codes_ref, adapt_refs, token_refs[0], *refs
            )
            frozen_kernel(
                2, depth, False, layout, True, place_ref, *token_refs, *piece_refs, *acc_refs,
                *out_refs,
            )

        *accs, low, b4, tok_t, codes_t = call(
            middle,
            [sds((tok_dev, half), F32)] * 2
            + low_outs
            + [sds((width_h, devices * seqs), BF16)],
            scratch=low_scratch
            + [
                pltpu.VMEM((seqs, rows, LANES), BF16),
                pltpu.VMEM((devices * seqs, LANES), F32),
            ],
            n_smem=2,
            n_in=5 + n_flat + n_adapt,
        )(place, task_share, task_codes, tokens, other_tokens, *flat, *accs, *adapt)
        sets = [([(last, far_pieces[last])], far_rows), ([(last, third_pieces[last])], third_rows)]
        theirs = frozen_call(place, depth, half, [other_tokens], None, sets, accs[1:])[0]
        mine = frozen_call(place, depth, half, [tokens], None, sets, accs[:1])[0]
    else:
        low, b4, tok_t = call(
            low_rank_body, low_outs, scratch=low_scratch, n_in=2, **low_cost
        )(adapt, tokens)
        own_half = lax.dynamic_slice_in_dim(frozen_weight, core * half, half, 1)
        order = jnp.arange(chips) ^ chip
        found = {0: own_half}
        for pieces, segments in ((near_pieces, near_rows), (far_pieces, far_rows)):
            joined = jnp.stack([pieces[m] for m in range(chips)])
            joined = jnp.take(joined, order, axis=0).transpose(1, 0, 2).reshape(-1, half)
            for k, _, size, row in segments:
                found[k] = joined[row : row + size]
        blocks = jnp.stack([found[k] for k in range(members)])
        weight = jnp.take(blocks, jnp.arange(members) ^ me_mp, axis=0).reshape(D, half)
        mine = jnp.dot(tokens, weight, preferred_element_type=F32)
        theirs = jnp.dot(other_tokens, weight, preferred_element_type=F32)
    received = xor_permute(theirs, "dp", 1)

    split = (devices, seqs, tiles, LANES)
    grads = call(
        functools.partial(backward_kernel, loss_scale),
        [sds(split if whole_tiles else (seqs, rows, LANES), BF16)],
        scratch=[
            pltpu.VMEM((tok_dev, KV), F32),
            pltpu.VMEM((B_ROWS, LANES), F32),
            pltpu.VMEM((seqs, rows, LANES), BF16),
        ],
        n_smem=4,
        n_in=6,
        flops=4 * tokens.size * LANES * seqs,
        nbytes=4 * tokens.size,
    )(place, task_share, seq_slot, token_counts, mine, received, teacher, low, b4, tok_t)[0]
    if not whole_tiles:
        grads = grads.reshape(seqs, devices, tiles, LANES).transpose(1, 0, 2, 3)
    routed = lax.all_to_all(grads, ("dp", "mp"), 0, 0, tiled=True)
    step = 8 if whole_tiles else tiles
    return pl.pallas_call(
        functools.partial(hyper_kernel, step),
        out_shape=sds((width_h, tiles * LANES), F32),
        in_specs=[pl.BlockSpec(memory_space=pltpu.VMEM)] * 2,
        out_specs=pl.BlockSpec(memory_space=pl.ANY),
        scratch_shapes=[
            pltpu.VMEM((devices * seqs * tiles, LANES), F32),
            pltpu.VMEM((width_h, tiles * LANES), F32),
            pltpu.SemaphoreType.DMA((tiles // step,)),
        ],
        compiler_params=pltpu.CompilerParams(vmem_limit_bytes=VMEM_LIMIT),
    )(codes_t, routed)


def solution(mesh):
    placed = (
        P(),
        P(None, ("dp", "mp")),
        P("mp", None),
        P(("dp", "mp"), None),
        P(("dp", "mp"), None),
        P(("dp", "mp")),
        P(),
        P(),
    )
    return jax.shard_map(
        shards, mesh=mesh, in_specs=placed, out_specs=P(None, ("dp", "mp")), check_vma=False
    )
```

```python
import functools
import math

import jax
import jax.numpy as jnp
from jax import lax
from jax.experimental import pallas as pl
from jax.experimental.pallas import tpu as pltpu
from jax.sharding import PartitionSpec as P

D = 5120
KV = 1024
R = 32
TPG = 4
SEQ_LEN = 128
LANES = 128
PACK = LANES // R
SLOT_ROWS = 16
A_ROWS = D * R // LANES
B_ROWS = R * KV // LANES
COL_TILES = KV // LANES
BLOCK_D = 512
BLOCK_Q = BLOCK_D // PACK
SHRINK = 1.0 / math.sqrt(D)
RANK_SCALE = 1.0 / math.sqrt(R)
F32 = jnp.float32
BF16 = jnp.bfloat16
VMEM_LIMIT = 16 * 1024 * 1024
ALL_VMEM = 56 * 1024 * 1024


def dot(a, b):
    return jnp.dot(a, b, preferred_element_type=F32)


def dot_nt(a, b):
    return lax.dot_general(a, b, (((1,), (1,)), ((), ())), preferred_element_type=F32)


def call(body, outs, scratch=(), n_smem=0, n_in=0, flops=0, nbytes=0, **kw):
    specs = [pl.BlockSpec(memory_space=pltpu.SMEM)] * n_smem
    specs += [pl.BlockSpec(memory_space=pltpu.VMEM)] * n_in
    out_specs = [pl.BlockSpec(memory_space=pltpu.VMEM)] * len(outs)
    return pl.pallas_call(
        body,
        out_shape=list(outs),
        in_specs=specs,
        out_specs=out_specs,
        scratch_shapes=list(scratch),
        compiler_params=pltpu.CompilerParams(vmem_limit_bytes=VMEM_LIMIT),
        cost_estimate=pl.CostEstimate(flops=flops, bytes_accessed=nbytes, transcendentals=0),
        **kw,
    )


def sds(shape, dtype):
    return jax.ShapeDtypeStruct(shape, dtype)


def xor_permute(array, axis, mask):
    return lax.ppermute(array, axis, [(i, i ^ mask) for i in range(lax.axis_size(axis))])


def chunk_kernel(place_ref, slot_hbm, weight_ref, near_ref, top_ref, bottom_ref, slot_ref, sems):
    depth = weight_ref.shape[0]
    width = near_ref.shape[1]
    mid = depth // 2
    half = weight_ref.shape[1] // 2
    at = pl.ds(pl.multiple_of(place_ref[1] * half + place_ref[2] * width, LANES), width)
    copies = [
        pltpu.make_async_copy(
            weight_ref.at[pl.ds(first, size), at], out.at[pl.ds(0, size), :], sems.at[i]
        )
        for i, (first, size, out) in enumerate(
            [(0, depth, near_ref), (0, mid, top_ref), (mid, mid, bottom_ref)]
        )
    ]
    for copy in copies:
        copy.start()
    slot_copy = pltpu.make_async_copy(slot_hbm, slot_ref, sems.at[3])
    slot_copy.start()
    slot_copy.wait()
    note = slot_note(slot_ref, width)
    near_ref[depth:, :] = note
    top_ref[mid:, :] = note
    bottom_ref[mid:, :] = note
    for copy in copies:
        copy.wait()


def slot_note(slot_ref, width):
    row = lax.broadcasted_iota(jnp.int32, (SLOT_ROWS, width), 0)
    note = jnp.zeros((SLOT_ROWS, width), jnp.int32)
    for s in range(slot_ref.shape[0]):
        note = jnp.where(row == s, slot_ref[s], note)
    return note.astype(F32).astype(BF16)


def adapters_kernel(tiles, share_ref, slot_ref, codes_ref, weight_ref, out_ref, scr):
    groups = out_ref.shape[0]
    rows = groups * TPG
    tasks = codes_ref.shape[0]
    row = lax.broadcasted_iota(jnp.int32, (rows, 1), 0)
    group, task = row // TPG, row % TPG
    live = jnp.zeros((rows, 1), jnp.int32)
    for g in range(groups):
        task = task + jnp.where(group > g, share_ref[g], 0)
        live = live + jnp.where(group == g, share_ref[g], 0)
    task = jnp.where(row % TPG < live, task, -1)
    pick = (task == lax.broadcasted_iota(jnp.int32, (rows, tasks), 1)).astype(BF16)
    chosen = dot(pick, codes_ref[...]).astype(BF16)
    for k in range(tiles):
        part = dot(chosen, weight_ref[:, k * LANES : (k + 1) * LANES])
        scr[pl.ds(k, rows, stride=tiles), :] = part
    note = slot_note(slot_ref, LANES)
    for g in range(groups):
        at = g * TPG * tiles
        out_ref[g, : TPG * tiles, :] = scr[at : at + TPG * tiles, :].astype(BF16)
        out_ref[g, TPG * tiles :, :] = note


def choose_kernel(tiles, slot_ref, near_ref, far_ref, got_ref, *out_refs):
    seqs = slot_ref.shape[0]
    groups = got_ref.shape[0]
    row = lax.broadcasted_iota(jnp.int32, (groups * seqs, LANES), 0)
    table = jnp.zeros((groups * seqs, LANES), F32)
    for g in range(groups):
        notes = got_ref[g, TPG * tiles :, :].astype(F32)
        for s in range(seqs):
            table = jnp.where(row == g * seqs + s, notes[s : s + 1, :], table)
    table = table.astype(BF16)
    far_rows = far_ref.shape[0]
    out_refs[1][:far_rows, :] = far_ref[...]
    note_ends = [None, (near_ref, near_ref.shape[0]), (far_ref, far_rows // 2), (far_ref, far_rows)]
    for k, out in enumerate(out_refs):
        if k > 0:
            note_ref, end = note_ends[k]
            notes = note_ref[end - SLOT_ROWS : end, :].astype(F32).astype(jnp.int32)
        if k == 1:
            out = out.at[far_rows:, :]
        for s in range(seqs):
            slot = slot_ref[s] if k == 0 else jnp.max(notes[s : s + 1, :])
            rows = pl.ds(pl.multiple_of(slot * tiles, 16), tiles)
            for g in range(groups):
                at = (g * seqs + s) * tiles
                out[at : at + tiles, :] = got_ref[g, rows, :]
        out[groups * seqs * tiles :, :] = table


def low_rank_kernel(
    tiles, place_ref, share_ref, codes_ref, adapt_refs, tokens_ref,
    low_ref, b4_ref, tok_t_ref, codes_t_ref, scr, held, table,
):
    n = len(adapt_refs)
    seqs = b4_ref.shape[0]
    groups = share_ref.shape[0]
    per_part = groups * seqs
    for k, part in enumerate(adapt_refs):
        part = part.at[part.shape[0] - per_part * (tiles + 1) :, :]
        table[k * per_part : (k + 1) * per_part, :] = part[per_part * tiles :, :].astype(F32)
        for g in range(groups):
            at = pl.multiple_of((g * n + (place_ref[0] ^ k)) * tiles, 16)
            for s in range(seqs):
                first = (g * seqs + s) * tiles
                held[s, pl.ds(at, tiles), :] = part[first : first + tiles, :]
    rows, tasks = table.shape[0], codes_ref.shape[0]
    task = table[:, :1].astype(jnp.int32)
    group = lax.broadcasted_iota(jnp.int32, (rows, 1), 0) % per_part // seqs
    for g in range(groups - 1):
        task = task + jnp.where(group > g, share_ref[g], 0)
    pick = (task == lax.broadcasted_iota(jnp.int32, (rows, tasks), 1)).astype(BF16)
    codes = dot(pick, codes_ref[...]).astype(BF16)
    at = lax.broadcasted_iota(jnp.int32, (rows, rows), 1)
    source = at % per_part // seqs * n + (place_ref[0] ^ (at // per_part))
    order = source * seqs + at % seqs == lax.broadcasted_iota(jnp.int32, (rows, rows), 0)
    codes_t_ref[...] = dot(order.astype(BF16), codes).T.astype(BF16)
    low_rank_body(held, tokens_ref, low_ref, b4_ref, tok_t_ref, scr)


def low_rank_body(adapt_ref, tokens_ref, low_ref, b4_ref, tok_t_ref, scr):
    seqs = b4_ref.shape[0]
    lane = lax.broadcasted_iota(jnp.int32, (BLOCK_D, LANES * seqs), 1)
    row = lax.broadcasted_iota(jnp.int32, (BLOCK_D, LANES * seqs), 0)
    keep = (lane % LANES) // R == row % PACK
    spread = (
        lax.broadcasted_iota(jnp.int32, (BLOCK_D, BLOCK_Q), 0) // PACK
        == lax.broadcasted_iota(jnp.int32, (BLOCK_D, BLOCK_Q), 1)
    ).astype(BF16)
    to = lax.broadcasted_iota(jnp.int32, (BLOCK_D, BLOCK_D), 0)
    sort = (
        to % BLOCK_Q * PACK + to // BLOCK_Q
        == lax.broadcasted_iota(jnp.int32, (BLOCK_D, BLOCK_D), 1)
    ).astype(BF16)
    acc = jnp.zeros((tokens_ref.shape[0], LANES * seqs), F32)
    for b in range(D // BLOCK_D):
        cols = slice(b * BLOCK_D, (b + 1) * BLOCK_D)
        part = jnp.concatenate(
            [adapt_ref[s, b * BLOCK_Q : (b + 1) * BLOCK_Q, :] for s in range(seqs)], axis=1
        )
        wide = jnp.where(keep, dot(spread, part), 0.0).astype(BF16)
        block = tokens_ref[:, cols]
        acc = acc + dot(block, wide)
        turned = dot_nt(sort, block).astype(BF16)
        for j in range(PACK):
            tok_t_ref[
                b * BLOCK_Q : (b + 1) * BLOCK_Q, j * block.shape[0] : (j + 1) * block.shape[0]
            ] = turned[j * BLOCK_Q : (j + 1) * BLOCK_Q, :]
    first = lax.broadcasted_iota(jnp.int32, (SEQ_LEN, LANES), 1) < R
    for s in range(seqs):
        z = acc[s * SEQ_LEN : (s + 1) * SEQ_LEN, s * LANES : (s + 1) * LANES]
        total = z
        for j in range(1, PACK):
            total = total + pltpu.roll(z, j * R, 1)
        low_ref[s * SEQ_LEN : (s + 1) * SEQ_LEN, :] = jnp.where(first, total * SHRINK, 0.0).astype(
            BF16
        )
        scr[...] = adapt_ref[s, A_ROWS:, :].astype(F32)
        for c in range(COL_TILES):
            piece = scr[pl.ds(c, R, stride=COL_TILES), :].astype(BF16)
            for j in range(PACK):
                b4_ref[s, j * R : (j + 1) * R, c * LANES : (c + 1) * LANES] = piece


def frozen_kernel(n_tok, depth, own, layout, has_acc, packed, place_ref, *refs):
    refs = iter(refs)
    token_refs = [next(refs) for _ in range(n_tok)]
    weight_ref = next(refs) if own else None
    sets = [
        ([(m, next(refs)) for m in masks], segments) for masks, segments in layout
    ]
    accs = [next(refs) for _ in range(n_tok)] if has_acc else [None] * n_tok
    outs = list(refs)
    me, core, chip = place_ref[0], place_ref[1], place_ref[2]
    width = sets[0][0][0][1].shape[1]

    def cols(k, first, size):
        if packed:
            return slice((k - packed) * depth + first, (k - packed) * depth + first + size)
        return pl.ds(pl.multiple_of((me ^ k) * depth + first, LANES), size)

    for tok, acc, out in zip(token_refs, accs, outs):
        if own:
            half = out.shape[1]
            block = weight_ref[:, pl.ds(pl.multiple_of(core * half, LANES), half)]
            out[...] = dot(tok[:, cols(0, 0, depth)], block)
        else:
            out[...] = acc[...]
        for pieces, segments in sets:
            for first_chip in range(0, len(pieces), 2):
                pair = pieces[first_chip : first_chip + 2]
                part = None
                for k, first, size, row in segments:
                    right = jnp.concatenate([x[row : row + size, :] for _, x in pair], axis=1)
                    term = dot(tok[:, cols(k, first, size)], right)
                    part = term if part is None else part + term
                for at, (mask, _) in enumerate(pair):
                    where = pl.ds(pl.multiple_of((chip ^ mask) * width, LANES), width)
                    out[:, where] += part[:, at * width : (at + 1) * width]


def frozen_layout(sets):
    layout = [([m for m, _ in pieces], segments) for pieces, segments in sets]
    return layout, [x for pieces, _ in sets for _, x in pieces]


def frozen_call(place, depth, half, tokens, weight, sets, accs, packed=0):
    rows = tokens[0].shape[0]
    layout, flat = frozen_layout(sets)
    size = 2 * rows * sum(x.size for x in flat) + (0 if weight is None else 2 * rows * depth * half)
    weights = [] if weight is None else [weight]
    return call(
        functools.partial(
            frozen_kernel, len(tokens), depth, weight is not None, layout, bool(accs), packed
        ),
        [sds((rows, half), F32)] * len(tokens),
        n_smem=1,
        n_in=len(tokens) + len(weights) + len(flat) + len(accs),
        flops=size * len(tokens),
        nbytes=2 * sum(x.size for x in flat) + 4 * rows * half * len(tokens),
    )(place, *tokens, *weights, *flat, *accs)


def backward_kernel(
    loss_scale, place_ref, share_ref, slot_ref, counts_ref, mine_ref, theirs_ref, teacher_ref, low_ref, b4_ref, tok_t_ref, out_ref,
    values, spaced, grads,
):
    seqs = b4_ref.shape[0]
    half = mine_ref.shape[1]
    core, group = place_ref[1], place_ref[3]
    n_tasks = counts_ref.shape[0]
    first_task = jnp.int32(0)
    for g in range(share_ref.shape[0]):
        first_task = first_task + jnp.where(g < group, share_ref[g], 0)
    all_counts = counts_ref[0]
    for t in range(1, n_tasks):
        all_counts = all_counts + counts_ref[t]
    values[:, pl.ds(pl.multiple_of(core * half, LANES), half)] = mine_ref[...]
    values[:, pl.ds(pl.multiple_of((1 - core) * half, LANES), half)] = theirs_ref[...]
    blocks = []
    for s in range(seqs):
        rows = slice(s * SEQ_LEN, (s + 1) * SEQ_LEN)
        low = low_ref[rows, :]
        b4 = b4_ref[s]
        error = values[rows, :] + dot(low, b4) * RANK_SCALE - teacher_ref[rows, :].astype(F32)
        count = jnp.full((1, KV), counts_ref[first_task + slot_ref[s]], jnp.int32).astype(F32)
        mean = jnp.full((1, KV), all_counts, jnp.int32).astype(F32) / n_tasks
        value_grad = (error * (mean / count * loss_scale)).astype(BF16)
        blocks.append((dot_nt(value_grad, b4) * RANK_SCALE).astype(BF16))
        second = dot(low.T, value_grad)[:R] * RANK_SCALE
        for c in range(COL_TILES):
            spaced[pl.ds(c, R, stride=COL_TILES), :] = second[:, c * LANES : (c + 1) * LANES]
        grads[s, A_ROWS:, :] = spaced[...].astype(BF16)
    zero = jnp.zeros_like(blocks[0])
    low_grad = jnp.concatenate(
        [
            jnp.concatenate([blocks[s] if s == i else zero for i in range(seqs)], axis=1)
            for s in range(seqs)
        ],
        axis=0,
    )
    group = lax.broadcasted_iota(jnp.int32, low_grad.shape, 1) % LANES // R
    low_grad = jnp.concatenate(
        [jnp.where(group == j, low_grad, jnp.zeros_like(low_grad)) for j in range(PACK)], axis=0
    )
    first = (dot(tok_t_ref[...], low_grad) * SHRINK).astype(BF16)
    for s in range(seqs):
        grads[s, :A_ROWS, :] = first[:, s * LANES : (s + 1) * LANES]
    store_grads(grads, out_ref)


def store_grads(grads, out_ref):
    if len(out_ref.shape) == 3:
        out_ref[...] = grads[...]
        return
    tiles = out_ref.shape[2]
    for i in range(out_ref.shape[0]):
        for s in range(out_ref.shape[1]):
            out_ref[i, s] = grads[s, i * tiles : (i + 1) * tiles, :]


def hyper_kernel(step, codes_t_ref, grads_ref, out_ref, scr, done, sems):
    devices, seqs, tiles, _ = grads_ref.shape
    rows = devices * seqs
    for i in range(devices):
        for s in range(seqs):
            at = (i * seqs + s) * tiles
            scr[at : at + tiles, :] = grads_ref[i, s].astype(F32)
    codes_t = codes_t_ref[...]
    copies = []
    for k in range(tiles):
        part = scr[pl.ds(k, rows, stride=tiles), :].astype(BF16)
        done[:, k * LANES : (k + 1) * LANES] = dot(codes_t, part)
        if (k + 1) % step == 0:
            cols = slice((k + 1 - step) * LANES, (k + 1) * LANES)
            copies.append(
                pltpu.make_async_copy(done.at[:, cols], out_ref.at[:, cols], sems.at[k // step])
            )
            copies[-1].start()
    for copy in copies:
        copy.wait()


def tied(*groups):
    return lax.optimization_barrier(groups)


def shards(
    task_codes, hyper_weight, frozen_weight, tokens, teacher, seq_slot, task_share, token_counts
):
    groups = lax.axis_size("dp")
    members = lax.axis_size("mp")
    devices = groups * members
    chips = groups // 2
    tok_dev = tokens.shape[0]
    seqs = seq_slot.shape[0]
    depth = frozen_weight.shape[0]
    tiles = hyper_weight.shape[1] // LANES
    rows = A_ROWS + B_ROWS
    width_h = task_codes.shape[1]
    loss_scale = 1.0 / math.sqrt(tok_dev * members)
    me_dp, me_mp = lax.axis_index("dp"), lax.axis_index("mp")
    core, chip = me_dp % 2, me_dp // 2
    place = jnp.stack([me_mp, core, chip, me_dp]).astype(jnp.int32)
    half = KV // 2
    width = half // chips
    whole_tiles = tiles % 16 == 0

    mid = depth // 2

    def direct(block):
        return {
            m: xor_permute(block, "dp", m << 1) if m else block
            for m in range(chips)
            if m & (m - 1) == 0
        }

    def forwarded(held, by_high):
        held = dict(held)
        for m in range(1, chips):
            if m not in held:
                bit = 1 << (m.bit_length() - 1) if by_high else m & -m
                held[m] = xor_permute(held[m ^ bit], "dp", bit << 1)
        return held

    other_tokens = xor_permute(tokens, "dp", 1)
    fits = width % LANES == 0 and mid % LANES == 0 and members == 4 and chips == 4
    fits = fits and whole_tiles and groups * seqs % 16 == 0
    near_rows = [(1, 0, depth, 0)]
    if fits:
        near, top, bottom = pl.pallas_call(
            chunk_kernel,
            in_specs=[pl.BlockSpec(memory_space=pltpu.SMEM)]
            + [pl.BlockSpec(memory_space=pltpu.HBM)] * 2,
            out_specs=[pl.BlockSpec(memory_space=pltpu.VMEM)] * 3,
            out_shape=[sds((n + SLOT_ROWS, width), BF16) for n in (depth, mid, mid)],
            scratch_shapes=[
                pltpu.SMEM(seq_slot.shape, jnp.int32),
                pltpu.SemaphoreType.DMA((4,)),
            ],
            compiler_params=pltpu.CompilerParams(vmem_limit_bytes=ALL_VMEM),
        )(place, seq_slot, frozen_weight)
        near, top, bottom, task_codes = tied(near, top, bottom, task_codes)
        other_tokens, task_codes = tied(other_tokens, task_codes)
        near = xor_permute(near, "mp", 1)
        top = xor_permute(top, "mp", 2)
        bottom = xor_permute(bottom, "mp", 3)
        near_held = direct(near)
        far = jnp.concatenate([top, bottom], axis=0)
        at = mid + SLOT_ROWS
        far_rows = [(2, 0, mid, 0), (3, mid, mid, at)]
        third_rows = [(3, 0, mid, 0), (2, mid, mid, at)]
    else:
        chunk = lax.dynamic_slice_in_dim(frozen_weight, core * half + chip * width, width, 1)
        near = xor_permute(chunk, "mp", 1)
        near_held = direct(near)
        far = jnp.concatenate(
            [xor_permute(chunk, "mp", k) for k in range(2, members)], axis=0
        )
        far_rows = [(k, 0, depth, (k - 2) * depth) for k in range(2, members)]

    if fits:
        sent = call(
            functools.partial(adapters_kernel, tiles),
            [sds((groups, TPG * tiles + SLOT_ROWS, LANES), BF16)],
            scratch=[pltpu.VMEM((groups * TPG * tiles, LANES), F32)],
            n_smem=2,
            n_in=2,
            flops=2 * groups * TPG * hyper_weight.size,
            nbytes=4 * hyper_weight.size,
        )(task_share, seq_slot, task_codes, hyper_weight)[0]
        got = lax.all_to_all(sent, "dp", 0, 0, tiled=True)
        chosen = call(
            functools.partial(choose_kernel, tiles),
            [
                sds((groups * seqs * (tiles + 1) + (far.shape[0] if k == 1 else 0), LANES), BF16)
                for k in range(members)
            ],
            n_smem=1,
            n_in=3,
            nbytes=8 * hyper_weight.size,
        )(seq_slot, near, far, got)
        near_held, far, chosen = tied(near_held, far, chosen)
        near_pieces = forwarded(near_held, True)
        adapt = [chosen[0]] + [xor_permute(chosen[k], "mp", k) for k in range(1, members)]
        third = adapt[1][: far.shape[0]]
    else:
        near_pieces = forwarded(near_held, True)
        slots = lax.all_to_all(
            jnp.broadcast_to(seq_slot[None], (devices, seqs)), ("dp", "mp"), 0, 0, tiled=True
        ).reshape(-1)
        offsets = jnp.cumsum(task_share) - task_share
        task_of = jnp.repeat(offsets, members * seqs) + slots
        pick = (jnp.arange(task_codes.shape[0])[:, None] == task_of[None, :]).astype(BF16)
        codes_t = dot(task_codes.T, pick).astype(BF16)
        sent = dot(codes_t.T, hyper_weight).astype(BF16).reshape(devices, seqs, tiles, LANES)
        adapt = lax.all_to_all(sent, ("dp", "mp"), 0, 0, tiled=True)
        adapt = adapt.transpose(1, 0, 2, 3).reshape(seqs, rows, LANES)

    far_held = direct(far)
    if fits:
        sets = [(list(near_held.items()), near_rows)]
        accs = frozen_call(place, depth, half, [tokens, other_tokens], frozen_weight, sets, [])
        last = chips - 1
        third, accs, near_last = tied(third, accs, near_pieces[last])
        third_held = direct(third)
        third_held, far_held, accs, adapt = tied(third_held, far_held, accs, adapt)
        third_pieces = forwarded(third_held, True)
    far_pieces = forwarded(far_held, False)

    low_outs = [
        sds((tok_dev, LANES), BF16),
        sds((seqs, LANES, KV), BF16),
        sds((D // PACK, PACK * tok_dev), BF16),
    ]
    low_cost = dict(
        flops=4 * tokens.size * LANES * seqs, nbytes=4 * tokens.size + 4 * seqs * rows * LANES
    )
    low_scratch = [pltpu.VMEM((B_ROWS, LANES), F32)]
    if fits:
        last = chips - 1
        sets = [
            ([(last, near_last)], near_rows),
            ([(m, far_held[m]) for m in far_held], far_rows),
            ([(m, third_held[m]) for m in third_held], third_rows),
        ]
        layout, flat = frozen_layout(sets)
        n_flat, n_adapt = len(flat), len(adapt)

        def middle(*refs):
            refs = list(refs)
            place_ref, share_ref, codes_ref = refs[:3]
            token_refs, refs = refs[3:5], refs[5:]
            piece_refs, refs = refs[:n_flat], refs[n_flat:]
            acc_refs, refs = refs[:2], refs[2:]
            adapt_refs, refs = refs[:n_adapt], refs[n_adapt:]
            out_refs, late_ref, refs = refs[:2], refs[2], refs[3:]
            for k in range(2, members):
                block = pl.ds(pl.multiple_of((place_ref[0] ^ k) * depth, LANES), depth)
                late_ref[:, (k - 2) * depth : (k - 1) * depth] = token_refs[1][:, block]
            low_rank_kernel(
                tiles, place_ref, share_ref, codes_ref, adapt_refs, token_refs[0], *refs
            )
            frozen_kernel(
                2, depth, False, layout, True, 0, place_ref, *token_refs, *piece_refs, *acc_refs,
                *out_refs,
            )

        *accs, late_tokens, low, b4, tok_t, codes_t = call(
            middle,
            [sds((tok_dev, half), F32)] * 2
            + [sds((tok_dev, (members - 2) * depth), BF16)]
            + low_outs
            + [sds((width_h, devices * seqs), BF16)],
            scratch=low_scratch
            + [
                pltpu.VMEM((seqs, rows, LANES), BF16),
                pltpu.VMEM((devices * seqs, LANES), F32),
            ],
            n_smem=2,
            n_in=5 + n_flat + n_adapt,
        )(place, task_share, task_codes, tokens, other_tokens, *flat, *accs, *adapt)
        sets = [([(last, far_pieces[last])], far_rows), ([(last, third_pieces[last])], third_rows)]
        theirs = frozen_call(place, depth, half, [late_tokens], None, sets, accs[1:], 2)[0]
        mine = frozen_call(place, depth, half, [tokens], None, sets, accs[:1])[0]
    else:
        low, b4, tok_t = call(
            low_rank_body, low_outs, scratch=low_scratch, n_in=2, **low_cost
        )(adapt, tokens)
        own_half = lax.dynamic_slice_in_dim(frozen_weight, core * half, half, 1)
        order = jnp.arange(chips) ^ chip
        found = {0: own_half}
        for pieces, segments in ((near_pieces, near_rows), (far_pieces, far_rows)):
            joined = jnp.stack([pieces[m] for m in range(chips)])
            joined = jnp.take(joined, order, axis=0).transpose(1, 0, 2).reshape(-1, half)
            for k, _, size, row in segments:
                found[k] = joined[row : row + size]
        blocks = jnp.stack([found[k] for k in range(members)])
        weight = jnp.take(blocks, jnp.arange(members) ^ me_mp, axis=0).reshape(D, half)
        mine = jnp.dot(tokens, weight, preferred_element_type=F32)
        theirs = jnp.dot(other_tokens, weight, preferred_element_type=F32)
    received = xor_permute(theirs, "dp", 1)

    split = (devices, seqs, tiles, LANES)
    grads = call(
        functools.partial(backward_kernel, loss_scale),
        [sds(split if whole_tiles else (seqs, rows, LANES), BF16)],
        scratch=[
            pltpu.VMEM((tok_dev, KV), F32),
            pltpu.VMEM((B_ROWS, LANES), F32),
            pltpu.VMEM((seqs, rows, LANES), BF16),
        ],
        n_smem=4,
        n_in=6,
        flops=4 * tokens.size * LANES * seqs,
        nbytes=4 * tokens.size,
    )(place, task_share, seq_slot, token_counts, mine, received, teacher, low, b4, tok_t)[0]
    if not whole_tiles:
        grads = grads.reshape(seqs, devices, tiles, LANES).transpose(1, 0, 2, 3)
    routed = lax.all_to_all(grads, ("dp", "mp"), 0, 0, tiled=True)
    step = 8 if whole_tiles else tiles
    return pl.pallas_call(
        functools.partial(hyper_kernel, step),
        out_shape=sds((width_h, tiles * LANES), F32),
        in_specs=[pl.BlockSpec(memory_space=pltpu.VMEM)] * 2,
        out_specs=pl.BlockSpec(memory_space=pl.ANY),
        scratch_shapes=[
            pltpu.VMEM((devices * seqs * tiles, LANES), F32),
            pltpu.VMEM((width_h, tiles * LANES), F32),
            pltpu.SemaphoreType.DMA((tiles // step,)),
        ],
        compiler_params=pltpu.CompilerParams(vmem_limit_bytes=VMEM_LIMIT),
    )(codes_t, routed)


def solution(mesh):
    placed = (
        P(),
        P(None, ("dp", "mp")),
        P("mp", None),
        P(("dp", "mp"), None),
        P(("dp", "mp"), None),
        P(("dp", "mp")),
        P(),
        P(),
    )
    return jax.shard_map(
        shards, mesh=mesh, in_specs=placed, out_specs=P(None, ("dp", "mp")), check_vma=False
    )
```

```python
import functools
import math

import jax
import jax.numpy as jnp
from jax import lax
from jax.experimental import pallas as pl
from jax.experimental.pallas import tpu as pltpu
from jax.sharding import PartitionSpec as P

D = 5120
KV = 1024
R = 32
TPG = 4
SEQ_LEN = 128
LANES = 128
PACK = LANES // R
SLOT_ROWS = 16
A_ROWS = D * R // LANES
B_ROWS = R * KV // LANES
COL_TILES = KV // LANES
BLOCK_D = 512
BLOCK_Q = BLOCK_D // PACK
SHRINK = 1.0 / math.sqrt(D)
RANK_SCALE = 1.0 / math.sqrt(R)
F32 = jnp.float32
BF16 = jnp.bfloat16
VMEM_LIMIT = 16 * 1024 * 1024
ALL_VMEM = 56 * 1024 * 1024


def dot(a, b):
    return jnp.dot(a, b, preferred_element_type=F32)


def dot_nt(a, b):
    return lax.dot_general(a, b, (((1,), (1,)), ((), ())), preferred_element_type=F32)


def call(body, outs, scratch=(), n_smem=0, n_in=0, flops=0, nbytes=0, **kw):
    specs = [pl.BlockSpec(memory_space=pltpu.SMEM)] * n_smem
    specs += [pl.BlockSpec(memory_space=pltpu.VMEM)] * n_in
    out_specs = [pl.BlockSpec(memory_space=pltpu.VMEM)] * len(outs)
    return pl.pallas_call(
        body,
        out_shape=list(outs),
        in_specs=specs,
        out_specs=out_specs,
        scratch_shapes=list(scratch),
        compiler_params=pltpu.CompilerParams(vmem_limit_bytes=VMEM_LIMIT),
        cost_estimate=pl.CostEstimate(flops=flops, bytes_accessed=nbytes, transcendentals=0),
        **kw,
    )


def sds(shape, dtype):
    return jax.ShapeDtypeStruct(shape, dtype)


def xor_permute(array, axis, mask):
    return lax.ppermute(array, axis, [(i, i ^ mask) for i in range(lax.axis_size(axis))])


def chunk_kernel(place_ref, slot_hbm, weight_ref, near_ref, top_ref, bottom_ref, slot_ref, sems):
    depth = weight_ref.shape[0]
    width = near_ref.shape[1]
    mid = depth // 2
    half = weight_ref.shape[1] // 2
    at = pl.ds(pl.multiple_of(place_ref[1] * half + place_ref[2] * width, LANES), width)
    copies = [
        pltpu.make_async_copy(
            weight_ref.at[pl.ds(first, size), at], out.at[pl.ds(0, size), :], sems.at[i]
        )
        for i, (first, size, out) in enumerate(
            [(0, depth, near_ref), (0, mid, top_ref), (mid, mid, bottom_ref)]
        )
    ]
    for copy in copies:
        copy.start()
    slot_copy = pltpu.make_async_copy(slot_hbm, slot_ref, sems.at[3])
    slot_copy.start()
    slot_copy.wait()
    note = slot_note(slot_ref, width)
    near_ref[depth:, :] = note
    top_ref[mid:, :] = note
    bottom_ref[mid:, :] = note
    for copy in copies:
        copy.wait()


def slot_note(slot_ref, width):
    row = lax.broadcasted_iota(jnp.int32, (SLOT_ROWS, width), 0)
    note = jnp.zeros((SLOT_ROWS, width), jnp.int32)
    for s in range(slot_ref.shape[0]):
        note = jnp.where(row == s, slot_ref[s], note)
    return note.astype(F32).astype(BF16)


def adapters_kernel(tiles, share_ref, slot_ref, codes_ref, weight_ref, out_ref, scr):
    groups = out_ref.shape[0]
    rows = groups * TPG
    tasks = codes_ref.shape[0]
    row = lax.broadcasted_iota(jnp.int32, (rows, 1), 0)
    group, task = row // TPG, row % TPG
    live = jnp.zeros((rows, 1), jnp.int32)
    for g in range(groups):
        task = task + jnp.where(group > g, share_ref[g], 0)
        live = live + jnp.where(group == g, share_ref[g], 0)
    task = jnp.where(row % TPG < live, task, -1)
    pick = (task == lax.broadcasted_iota(jnp.int32, (rows, tasks), 1)).astype(BF16)
    chosen = dot(pick, codes_ref[...]).astype(BF16)
    for k in range(tiles):
        part = dot(chosen, weight_ref[:, k * LANES : (k + 1) * LANES])
        scr[pl.ds(k, rows, stride=tiles), :] = part
    note = slot_note(slot_ref, LANES)
    for g in range(groups):
        at = g * TPG * tiles
        out_ref[g, : TPG * tiles, :] = scr[at : at + TPG * tiles, :].astype(BF16)
        out_ref[g, TPG * tiles :, :] = note


def choose_kernel(tiles, slot_ref, near_ref, far_ref, got_ref, *out_refs):
    seqs = slot_ref.shape[0]
    groups = got_ref.shape[0]
    row = lax.broadcasted_iota(jnp.int32, (groups * seqs, LANES), 0)
    table = jnp.zeros((groups * seqs, LANES), F32)
    for g in range(groups):
        notes = got_ref[g, TPG * tiles :, :].astype(F32)
        for s in range(seqs):
            table = jnp.where(row == g * seqs + s, notes[s : s + 1, :], table)
    table = table.astype(BF16)
    far_rows = far_ref.shape[0]
    out_refs[1][:far_rows, :] = far_ref[...]
    note_ends = [None, (near_ref, near_ref.shape[0]), (far_ref, far_rows // 2), (far_ref, far_rows)]
    for k, out in enumerate(out_refs):
        if k > 0:
            note_ref, end = note_ends[k]
            notes = note_ref[end - SLOT_ROWS : end, :].astype(F32).astype(jnp.int32)
        if k == 1:
            out = out.at[far_rows:, :]
        for s in range(seqs):
            slot = slot_ref[s] if k == 0 else jnp.max(notes[s : s + 1, :])
            rows = pl.ds(pl.multiple_of(slot * tiles, 16), tiles)
            for g in range(groups):
                at = (g * seqs + s) * tiles
                out[at : at + tiles, :] = got_ref[g, rows, :]
        out[groups * seqs * tiles :, :] = table


def low_rank_kernel(
    tiles, place_ref, share_ref, codes_ref, adapt_refs, tokens_ref,
    low_ref, b4_ref, codes_t_ref, scr, held, table,
):
    n = len(adapt_refs)
    seqs = b4_ref.shape[0]
    groups = share_ref.shape[0]
    per_part = groups * seqs
    for k, part in enumerate(adapt_refs):
        part = part.at[part.shape[0] - per_part * (tiles + 1) :, :]
        table[k * per_part : (k + 1) * per_part, :] = part[per_part * tiles :, :].astype(F32)
        for g in range(groups):
            at = pl.multiple_of((g * n + (place_ref[0] ^ k)) * tiles, 16)
            for s in range(seqs):
                first = (g * seqs + s) * tiles
                held[s, pl.ds(at, tiles), :] = part[first : first + tiles, :]
    rows, tasks = table.shape[0], codes_ref.shape[0]
    task = table[:, :1].astype(jnp.int32)
    group = lax.broadcasted_iota(jnp.int32, (rows, 1), 0) % per_part // seqs
    for g in range(groups - 1):
        task = task + jnp.where(group > g, share_ref[g], 0)
    pick = (task == lax.broadcasted_iota(jnp.int32, (rows, tasks), 1)).astype(BF16)
    codes = dot(pick, codes_ref[...]).astype(BF16)
    at = lax.broadcasted_iota(jnp.int32, (rows, rows), 1)
    source = at % per_part // seqs * n + (place_ref[0] ^ (at // per_part))
    order = source * seqs + at % seqs == lax.broadcasted_iota(jnp.int32, (rows, rows), 0)
    codes_t_ref[...] = dot(order.astype(BF16), codes).T.astype(BF16)
    low_rank_body(held, tokens_ref, low_ref, b4_ref, scr)


def turn_tokens(tokens_ref, tok_t_ref):
    to = lax.broadcasted_iota(jnp.int32, (BLOCK_D, BLOCK_D), 0)
    sort = (
        to % BLOCK_Q * PACK + to // BLOCK_Q
        == lax.broadcasted_iota(jnp.int32, (BLOCK_D, BLOCK_D), 1)
    ).astype(BF16)
    for b in range(D // BLOCK_D):
        block = tokens_ref[:, b * BLOCK_D : (b + 1) * BLOCK_D]
        turned = dot_nt(sort, block).astype(BF16)
        for j in range(PACK):
            tok_t_ref[
                b * BLOCK_Q : (b + 1) * BLOCK_Q, j * block.shape[0] : (j + 1) * block.shape[0]
            ] = turned[j * BLOCK_Q : (j + 1) * BLOCK_Q, :]


def low_rank_body(adapt_ref, tokens_ref, low_ref, b4_ref, scr):
    seqs = b4_ref.shape[0]
    lane = lax.broadcasted_iota(jnp.int32, (BLOCK_D, LANES * seqs), 1)
    row = lax.broadcasted_iota(jnp.int32, (BLOCK_D, LANES * seqs), 0)
    keep = (lane % LANES) // R == row % PACK
    spread = (
        lax.broadcasted_iota(jnp.int32, (BLOCK_D, BLOCK_Q), 0) // PACK
        == lax.broadcasted_iota(jnp.int32, (BLOCK_D, BLOCK_Q), 1)
    ).astype(BF16)
    acc = jnp.zeros((tokens_ref.shape[0], LANES * seqs), F32)
    for b in range(D // BLOCK_D):
        cols = slice(b * BLOCK_D, (b + 1) * BLOCK_D)
        part = jnp.concatenate(
            [adapt_ref[s, b * BLOCK_Q : (b + 1) * BLOCK_Q, :] for s in range(seqs)], axis=1
        )
        wide = jnp.where(keep, dot(spread, part), 0.0).astype(BF16)
        block = tokens_ref[:, cols]
        acc = acc + dot(block, wide)
    first = lax.broadcasted_iota(jnp.int32, (SEQ_LEN, LANES), 1) < R
    for s in range(seqs):
        z = acc[s * SEQ_LEN : (s + 1) * SEQ_LEN, s * LANES : (s + 1) * LANES]
        total = z
        for j in range(1, PACK):
            total = total + pltpu.roll(z, j * R, 1)
        low_ref[s * SEQ_LEN : (s + 1) * SEQ_LEN, :] = jnp.where(first, total * SHRINK, 0.0).astype(
            BF16
        )
        scr[...] = adapt_ref[s, A_ROWS:, :].astype(F32)
        for c in range(COL_TILES):
            piece = scr[pl.ds(c, R, stride=COL_TILES), :].astype(BF16)
            for j in range(PACK):
                b4_ref[s, j * R : (j + 1) * R, c * LANES : (c + 1) * LANES] = piece


def frozen_kernel(n_tok, depth, own, layout, has_acc, packed, place_ref, *refs):
    refs = iter(refs)
    token_refs = [next(refs) for _ in range(n_tok)]
    weight_ref = next(refs) if own else None
    sets = [
        ([(m, next(refs)) for m in masks], segments) for masks, segments in layout
    ]
    accs = [next(refs) for _ in range(n_tok)] if has_acc else [None] * n_tok
    outs = list(refs)
    me, core, chip = place_ref[0], place_ref[1], place_ref[2]
    width = sets[0][0][0][1].shape[1]

    def cols(k, first, size):
        if packed:
            return slice((k - packed) * depth + first, (k - packed) * depth + first + size)
        return pl.ds(pl.multiple_of((me ^ k) * depth + first, LANES), size)

    for tok, acc, out in zip(token_refs, accs, outs):
        if own:
            half = out.shape[1]
            block = weight_ref[:, pl.ds(pl.multiple_of(core * half, LANES), half)]
            out[...] = dot(tok[:, cols(0, 0, depth)], block)
        else:
            out[...] = acc[...]
        for pieces, segments in sets:
            for first_chip in range(0, len(pieces), 2):
                pair = pieces[first_chip : first_chip + 2]
                part = None
                for k, first, size, row in segments:
                    right = jnp.concatenate([x[row : row + size, :] for _, x in pair], axis=1)
                    term = dot(tok[:, cols(k, first, size)], right)
                    part = term if part is None else part + term
                for at, (mask, _) in enumerate(pair):
                    where = pl.ds(pl.multiple_of((chip ^ mask) * width, LANES), width)
                    out[:, where] += part[:, at * width : (at + 1) * width]


def frozen_layout(sets):
    layout = [([m for m, _ in pieces], segments) for pieces, segments in sets]
    return layout, [x for pieces, _ in sets for _, x in pieces]


def frozen_call(place, depth, half, tokens, weight, sets, accs, packed=0):
    rows = tokens[0].shape[0]
    layout, flat = frozen_layout(sets)
    size = 2 * rows * sum(x.size for x in flat) + (0 if weight is None else 2 * rows * depth * half)
    weights = [] if weight is None else [weight]
    return call(
        functools.partial(
            frozen_kernel, len(tokens), depth, weight is not None, layout, bool(accs), packed
        ),
        [sds((rows, half), F32)] * len(tokens),
        n_smem=1,
        n_in=len(tokens) + len(weights) + len(flat) + len(accs),
        flops=size * len(tokens),
        nbytes=2 * sum(x.size for x in flat) + 4 * rows * half * len(tokens),
    )(place, *tokens, *weights, *flat, *accs)


def backward_kernel(
    loss_scale, place_ref, share_ref, slot_ref, counts_ref, mine_ref, theirs_ref, teacher_ref, low_ref, b4_ref, tok_t_ref, out_ref,
    values, spaced, grads,
):
    seqs = b4_ref.shape[0]
    half = mine_ref.shape[1]
    core, group = place_ref[1], place_ref[3]
    n_tasks = counts_ref.shape[0]
    first_task = jnp.int32(0)
    for g in range(share_ref.shape[0]):
        first_task = first_task + jnp.where(g < group, share_ref[g], 0)
    all_counts = counts_ref[0]
    for t in range(1, n_tasks):
        all_counts = all_counts + counts_ref[t]
    values[:, pl.ds(pl.multiple_of(core * half, LANES), half)] = mine_ref[...]
    values[:, pl.ds(pl.multiple_of((1 - core) * half, LANES), half)] = theirs_ref[...]
    blocks = []
    for s in range(seqs):
        rows = slice(s * SEQ_LEN, (s + 1) * SEQ_LEN)
        low = low_ref[rows, :]
        b4 = b4_ref[s]
        error = values[rows, :] + dot(low, b4) * RANK_SCALE - teacher_ref[rows, :].astype(F32)
        count = jnp.full((1, KV), counts_ref[first_task + slot_ref[s]], jnp.int32).astype(F32)
        mean = jnp.full((1, KV), all_counts, jnp.int32).astype(F32) / n_tasks
        value_grad = (error * (mean / count * loss_scale)).astype(BF16)
        blocks.append((dot_nt(value_grad, b4) * RANK_SCALE).astype(BF16))
        second = dot(low.T, value_grad)[:R] * RANK_SCALE
        for c in range(COL_TILES):
            spaced[pl.ds(c, R, stride=COL_TILES), :] = second[:, c * LANES : (c + 1) * LANES]
        grads[s, A_ROWS:, :] = spaced[...].astype(BF16)
    zero = jnp.zeros_like(blocks[0])
    low_grad = jnp.concatenate(
        [
            jnp.concatenate([blocks[s] if s == i else zero for i in range(seqs)], axis=1)
            for s in range(seqs)
        ],
        axis=0,
    )
    group = lax.broadcasted_iota(jnp.int32, low_grad.shape, 1) % LANES // R
    low_grad = jnp.concatenate(
        [jnp.where(group == j, low_grad, jnp.zeros_like(low_grad)) for j in range(PACK)], axis=0
    )
    first = (dot(tok_t_ref[...], low_grad) * SHRINK).astype(BF16)
    for s in range(seqs):
        grads[s, :A_ROWS, :] = first[:, s * LANES : (s + 1) * LANES]
    store_grads(grads, out_ref)


def store_grads(grads, out_ref):
    if len(out_ref.shape) == 3:
        out_ref[...] = grads[...]
        return
    tiles = out_ref.shape[2]
    for i in range(out_ref.shape[0]):
        for s in range(out_ref.shape[1]):
            out_ref[i, s] = grads[s, i * tiles : (i + 1) * tiles, :]


def hyper_kernel(step, codes_t_ref, grads_ref, out_ref, scr, done, sems):
    devices, seqs, tiles, _ = grads_ref.shape
    rows = devices * seqs
    for i in range(devices):
        for s in range(seqs):
            at = (i * seqs + s) * tiles
            scr[at : at + tiles, :] = grads_ref[i, s].astype(F32)
    codes_t = codes_t_ref[...]
    copies = []
    for k in range(tiles):
        part = scr[pl.ds(k, rows, stride=tiles), :].astype(BF16)
        done[:, k * LANES : (k + 1) * LANES] = dot(codes_t, part)
        if (k + 1) % step == 0:
            cols = slice((k + 1 - step) * LANES, (k + 1) * LANES)
            copies.append(
                pltpu.make_async_copy(done.at[:, cols], out_ref.at[:, cols], sems.at[k // step])
            )
            copies[-1].start()
    for copy in copies:
        copy.wait()


def tied(*groups):
    return lax.optimization_barrier(groups)


def shards(
    task_codes, hyper_weight, frozen_weight, tokens, teacher, seq_slot, task_share, token_counts
):
    groups = lax.axis_size("dp")
    members = lax.axis_size("mp")
    devices = groups * members
    chips = groups // 2
    tok_dev = tokens.shape[0]
    seqs = seq_slot.shape[0]
    depth = frozen_weight.shape[0]
    tiles = hyper_weight.shape[1] // LANES
    rows = A_ROWS + B_ROWS
    width_h = task_codes.shape[1]
    loss_scale = 1.0 / math.sqrt(tok_dev * members)
    me_dp, me_mp = lax.axis_index("dp"), lax.axis_index("mp")
    core, chip = me_dp % 2, me_dp // 2
    place = jnp.stack([me_mp, core, chip, me_dp]).astype(jnp.int32)
    half = KV // 2
    width = half // chips
    whole_tiles = tiles % 16 == 0

    mid = depth // 2

    def direct(block):
        return {
            m: xor_permute(block, "dp", m << 1) if m else block
            for m in range(chips)
            if m & (m - 1) == 0
        }

    def forwarded(held, by_high):
        held = dict(held)
        for m in range(1, chips):
            if m not in held:
                bit = 1 << (m.bit_length() - 1) if by_high else m & -m
                held[m] = xor_permute(held[m ^ bit], "dp", bit << 1)
        return held

    other_tokens = xor_permute(tokens, "dp", 1)
    fits = width % LANES == 0 and mid % LANES == 0 and members == 4 and chips == 4
    fits = fits and whole_tiles and groups * seqs % 16 == 0
    near_rows = [(1, 0, depth, 0)]
    if fits:
        near, top, bottom = pl.pallas_call(
            chunk_kernel,
            in_specs=[pl.BlockSpec(memory_space=pltpu.SMEM)]
            + [pl.BlockSpec(memory_space=pltpu.HBM)] * 2,
            out_specs=[pl.BlockSpec(memory_space=pltpu.VMEM)] * 3,
            out_shape=[sds((n + SLOT_ROWS, width), BF16) for n in (depth, mid, mid)],
            scratch_shapes=[
                pltpu.SMEM(seq_slot.shape, jnp.int32),
                pltpu.SemaphoreType.DMA((4,)),
            ],
            compiler_params=pltpu.CompilerParams(vmem_limit_bytes=ALL_VMEM),
        )(place, seq_slot, frozen_weight)
        near, top, bottom, task_codes = tied(near, top, bottom, task_codes)
        other_tokens, task_codes = tied(other_tokens, task_codes)
        near = xor_permute(near, "mp", 1)
        top = xor_permute(top, "mp", 2)
        bottom = xor_permute(bottom, "mp", 3)
        near_held = direct(near)
        far = jnp.concatenate([top, bottom], axis=0)
        at = mid + SLOT_ROWS
        far_rows = [(2, 0, mid, 0), (3, mid, mid, at)]
        third_rows = [(3, 0, mid, 0), (2, mid, mid, at)]
    else:
        chunk = lax.dynamic_slice_in_dim(frozen_weight, core * half + chip * width, width, 1)
        near = xor_permute(chunk, "mp", 1)
        near_held = direct(near)
        far = jnp.concatenate(
            [xor_permute(chunk, "mp", k) for k in range(2, members)], axis=0
        )
        far_rows = [(k, 0, depth, (k - 2) * depth) for k in range(2, members)]

    if fits:
        sent = call(
            functools.partial(adapters_kernel, tiles),
            [sds((groups, TPG * tiles + SLOT_ROWS, LANES), BF16)],
            scratch=[pltpu.VMEM((groups * TPG * tiles, LANES), F32)],
            n_smem=2,
            n_in=2,
            flops=2 * groups * TPG * hyper_weight.size,
            nbytes=4 * hyper_weight.size,
        )(task_share, seq_slot, task_codes, hyper_weight)[0]
        got = lax.all_to_all(sent, "dp", 0, 0, tiled=True)
        chosen = call(
            functools.partial(choose_kernel, tiles),
            [
                sds((groups * seqs * (tiles + 1) + (far.shape[0] if k == 1 else 0), LANES), BF16)
                for k in range(members)
            ],
            n_smem=1,
            n_in=3,
            nbytes=8 * hyper_weight.size,
        )(seq_slot, near, far, got)
        near_held, far, chosen = tied(near_held, far, chosen)
        near_pieces = forwarded(near_held, True)
        adapt = [chosen[0]] + [xor_permute(chosen[k], "mp", k) for k in range(1, members)]
        third = adapt[1][: far.shape[0]]
    else:
        near_pieces = forwarded(near_held, True)
        slots = lax.all_to_all(
            jnp.broadcast_to(seq_slot[None], (devices, seqs)), ("dp", "mp"), 0, 0, tiled=True
        ).reshape(-1)
        offsets = jnp.cumsum(task_share) - task_share
        task_of = jnp.repeat(offsets, members * seqs) + slots
        pick = (jnp.arange(task_codes.shape[0])[:, None] == task_of[None, :]).astype(BF16)
        codes_t = dot(task_codes.T, pick).astype(BF16)
        sent = dot(codes_t.T, hyper_weight).astype(BF16).reshape(devices, seqs, tiles, LANES)
        adapt = lax.all_to_all(sent, ("dp", "mp"), 0, 0, tiled=True)
        adapt = adapt.transpose(1, 0, 2, 3).reshape(seqs, rows, LANES)

    low_outs = [
        sds((tok_dev, LANES), BF16),
        sds((seqs, LANES, KV), BF16),
    ]
    turned = sds((D // PACK, PACK * tok_dev), BF16)
    far_held = direct(far)
    if fits:
        sets = [(list(near_held.items()), near_rows)]
        early_layout, flat = frozen_layout(sets)

        def early(place_ref, *refs):
            *refs, tok_t_ref = refs
            turn_tokens(refs[0], tok_t_ref)
            frozen_kernel(2, depth, True, early_layout, False, 0, place_ref, *refs)

        *accs, tok_t = call(
            early,
            [sds((tok_dev, half), F32)] * 2 + [turned],
            n_smem=1,
            n_in=3 + len(flat),
        )(place, tokens, other_tokens, frozen_weight, *flat)
        last = chips - 1
        third, accs, near_last = tied(third, accs, near_pieces[last])
        third_held = direct(third)
        third_held, far_held, accs, adapt = tied(third_held, far_held, accs, adapt)
        third_pieces = forwarded(third_held, True)
    far_pieces = forwarded(far_held, False)

    low_cost = dict(
        flops=4 * tokens.size * LANES * seqs, nbytes=4 * tokens.size + 4 * seqs * rows * LANES
    )
    low_scratch = [pltpu.VMEM((B_ROWS, LANES), F32)]
    if fits:
        last = chips - 1
        sets = [
            ([(last, near_last)], near_rows),
            ([(m, far_held[m]) for m in far_held], far_rows),
            ([(m, third_held[m]) for m in third_held], third_rows),
        ]
        layout, flat = frozen_layout(sets)
        n_flat, n_adapt = len(flat), len(adapt)

        def middle(*refs):
            refs = list(refs)
            place_ref, share_ref, codes_ref = refs[:3]
            token_refs, refs = refs[3:5], refs[5:]
            piece_refs, refs = refs[:n_flat], refs[n_flat:]
            acc_refs, refs = refs[:2], refs[2:]
            adapt_refs, refs = refs[:n_adapt], refs[n_adapt:]
            out_refs, late_ref, refs = refs[:2], refs[2], refs[3:]
            for k in range(2, members):
                block = pl.ds(pl.multiple_of((place_ref[0] ^ k) * depth, LANES), depth)
                late_ref[:, (k - 2) * depth : (k - 1) * depth] = token_refs[1][:, block]
            low_rank_kernel(
                tiles, place_ref, share_ref, codes_ref, adapt_refs, token_refs[0], *refs
            )
            frozen_kernel(
                2, depth, False, layout, True, 0, place_ref, *token_refs, *piece_refs, *acc_refs,
                *out_refs,
            )

        *accs, late_tokens, low, b4, codes_t = call(
            middle,
            [sds((tok_dev, half), F32)] * 2
            + [sds((tok_dev, (members - 2) * depth), BF16)]
            + low_outs
            + [sds((width_h, devices * seqs), BF16)],
            scratch=low_scratch
            + [
                pltpu.VMEM((seqs, rows, LANES), BF16),
                pltpu.VMEM((devices * seqs, LANES), F32),
            ],
            n_smem=2,
            n_in=5 + n_flat + n_adapt,
        )(place, task_share, task_codes, tokens, other_tokens, *flat, *accs, *adapt)
        sets = [([(last, far_pieces[last])], far_rows), ([(last, third_pieces[last])], third_rows)]
        theirs = frozen_call(place, depth, half, [late_tokens], None, sets, accs[1:], 2)[0]
        mine = frozen_call(place, depth, half, [tokens], None, sets, accs[:1])[0]
    else:
        low, b4 = call(low_rank_body, low_outs, scratch=low_scratch, n_in=2, **low_cost)(
            adapt, tokens
        )
        tok_t = call(turn_tokens, [turned], n_in=1)(tokens)[0]
        own_half = lax.dynamic_slice_in_dim(frozen_weight, core * half, half, 1)
        order = jnp.arange(chips) ^ chip
        found = {0: own_half}
        for pieces, segments in ((near_pieces, near_rows), (far_pieces, far_rows)):
            joined = jnp.stack([pieces[m] for m in range(chips)])
            joined = jnp.take(joined, order, axis=0).transpose(1, 0, 2).reshape(-1, half)
            for k, _, size, row in segments:
                found[k] = joined[row : row + size]
        blocks = jnp.stack([found[k] for k in range(members)])
        weight = jnp.take(blocks, jnp.arange(members) ^ me_mp, axis=0).reshape(D, half)
        mine = jnp.dot(tokens, weight, preferred_element_type=F32)
        theirs = jnp.dot(other_tokens, weight, preferred_element_type=F32)
    received = xor_permute(theirs, "dp", 1)

    split = (devices, seqs, tiles, LANES)
    grads = call(
        functools.partial(backward_kernel, loss_scale),
        [sds(split if whole_tiles else (seqs, rows, LANES), BF16)],
        scratch=[
            pltpu.VMEM((tok_dev, KV), F32),
            pltpu.VMEM((B_ROWS, LANES), F32),
            pltpu.VMEM((seqs, rows, LANES), BF16),
        ],
        n_smem=4,
        n_in=6,
        flops=4 * tokens.size * LANES * seqs,
        nbytes=4 * tokens.size,
    )(place, task_share, seq_slot, token_counts, mine, received, teacher, low, b4, tok_t)[0]
    if not whole_tiles:
        grads = grads.reshape(seqs, devices, tiles, LANES).transpose(1, 0, 2, 3)
    routed = lax.all_to_all(grads, ("dp", "mp"), 0, 0, tiled=True)
    step = 8 if whole_tiles else tiles
    return pl.pallas_call(
        functools.partial(hyper_kernel, step),
        out_shape=sds((width_h, tiles * LANES), F32),
        in_specs=[pl.BlockSpec(memory_space=pltpu.VMEM)] * 2,
        out_specs=pl.BlockSpec(memory_space=pl.ANY),
        scratch_shapes=[
            pltpu.VMEM((devices * seqs * tiles, LANES), F32),
            pltpu.VMEM((width_h, tiles * LANES), F32),
            pltpu.SemaphoreType.DMA((tiles // step,)),
        ],
        compiler_params=pltpu.CompilerParams(vmem_limit_bytes=VMEM_LIMIT),
    )(codes_t, routed)


def solution(mesh):
    placed = (
        P(),
        P(None, ("dp", "mp")),
        P("mp", None),
        P(("dp", "mp"), None),
        P(("dp", "mp"), None),
        P(("dp", "mp")),
        P(),
        P(),
    )
    return jax.shard_map(
        shards, mesh=mesh, in_specs=placed, out_specs=P(None, ("dp", "mp")), check_vma=False
    )
```

```python
import functools
import math

import jax
import jax.numpy as jnp
from jax import lax
from jax.experimental import pallas as pl
from jax.experimental.pallas import tpu as pltpu
from jax.sharding import PartitionSpec as P

D = 5120
KV = 1024
R = 32
TPG = 4
SEQ_LEN = 128
LANES = 128
PACK = LANES // R
SLOT_ROWS = 16
A_ROWS = D * R // LANES
B_ROWS = R * KV // LANES
COL_TILES = KV // LANES
BLOCK_D = 512
BLOCK_Q = BLOCK_D // PACK
SHRINK = 1.0 / math.sqrt(D)
RANK_SCALE = 1.0 / math.sqrt(R)
F32 = jnp.float32
BF16 = jnp.bfloat16
VMEM_LIMIT = 16 * 1024 * 1024
ALL_VMEM = 56 * 1024 * 1024


def dot(a, b):
    return jnp.dot(a, b, preferred_element_type=F32)


def dot_nt(a, b):
    return lax.dot_general(a, b, (((1,), (1,)), ((), ())), preferred_element_type=F32)


def call(body, outs, scratch=(), n_smem=0, n_in=0, flops=0, nbytes=0, **kw):
    specs = [pl.BlockSpec(memory_space=pltpu.SMEM)] * n_smem
    specs += [pl.BlockSpec(memory_space=pltpu.VMEM)] * n_in
    out_specs = [pl.BlockSpec(memory_space=pltpu.VMEM)] * len(outs)
    return pl.pallas_call(
        body,
        out_shape=list(outs),
        in_specs=specs,
        out_specs=out_specs,
        scratch_shapes=list(scratch),
        compiler_params=pltpu.CompilerParams(vmem_limit_bytes=VMEM_LIMIT),
        cost_estimate=pl.CostEstimate(flops=flops, bytes_accessed=nbytes, transcendentals=0),
        **kw,
    )


def sds(shape, dtype):
    return jax.ShapeDtypeStruct(shape, dtype)


def xor_permute(array, axis, mask):
    return lax.ppermute(array, axis, [(i, i ^ mask) for i in range(lax.axis_size(axis))])


def chunk_kernel(place_ref, slot_hbm, weight_ref, near_ref, top_ref, bottom_ref, slot_ref, sems):
    depth = weight_ref.shape[0]
    width = near_ref.shape[1]
    mid = depth // 2
    half = weight_ref.shape[1] // 2
    at = pl.ds(pl.multiple_of(place_ref[1] * half + place_ref[2] * width, LANES), width)
    copies = [
        pltpu.make_async_copy(
            weight_ref.at[pl.ds(first, size), at], out.at[pl.ds(0, size), :], sems.at[i]
        )
        for i, (first, size, out) in enumerate(
            [(0, depth, near_ref), (0, mid, top_ref), (mid, mid, bottom_ref)]
        )
    ]
    for copy in copies:
        copy.start()
    slot_copy = pltpu.make_async_copy(slot_hbm, slot_ref, sems.at[3])
    slot_copy.start()
    slot_copy.wait()
    note = slot_note(slot_ref, width)
    near_ref[depth:, :] = note
    top_ref[mid:, :] = note
    bottom_ref[mid:, :] = note
    for copy in copies:
        copy.wait()


def slot_note(slot_ref, width):
    row = lax.broadcasted_iota(jnp.int32, (SLOT_ROWS, width), 0)
    note = jnp.zeros((SLOT_ROWS, width), jnp.int32)
    for s in range(slot_ref.shape[0]):
        note = jnp.where(row == s, slot_ref[s], note)
    return note.astype(F32).astype(BF16)


def adapters_kernel(tiles, share_ref, slot_ref, codes_ref, weight_ref, out_ref, scr):
    groups = out_ref.shape[0]
    rows = groups * TPG
    tasks = codes_ref.shape[0]
    row = lax.broadcasted_iota(jnp.int32, (rows, 1), 0)
    group, task = row // TPG, row % TPG
    live = jnp.zeros((rows, 1), jnp.int32)
    for g in range(groups):
        task = task + jnp.where(group > g, share_ref[g], 0)
        live = live + jnp.where(group == g, share_ref[g], 0)
    task = jnp.where(row % TPG < live, task, -1)
    pick = (task == lax.broadcasted_iota(jnp.int32, (rows, tasks), 1)).astype(BF16)
    chosen = dot(pick, codes_ref[...]).astype(BF16)
    for k in range(tiles):
        part = dot(chosen, weight_ref[:, k * LANES : (k + 1) * LANES])
        scr[pl.ds(k, rows, stride=tiles), :] = part
    note = slot_note(slot_ref, LANES)
    for g in range(groups):
        at = g * TPG * tiles
        out_ref[g, : TPG * tiles, :] = scr[at : at + TPG * tiles, :].astype(BF16)
        out_ref[g, TPG * tiles :, :] = note


def choose_kernel(tiles, slot_ref, near_ref, far_ref, got_ref, *out_refs):
    seqs = slot_ref.shape[0]
    groups = got_ref.shape[0]
    row = lax.broadcasted_iota(jnp.int32, (groups * seqs, LANES), 0)
    table = jnp.zeros((groups * seqs, LANES), F32)
    for g in range(groups):
        notes = got_ref[g, TPG * tiles :, :].astype(F32)
        for s in range(seqs):
            table = jnp.where(row == g * seqs + s, notes[s : s + 1, :], table)
    table = table.astype(BF16)
    far_rows = far_ref.shape[0]
    out_refs[1][:far_rows, :] = far_ref[...]
    note_ends = [None, (near_ref, near_ref.shape[0]), (far_ref, far_rows // 2), (far_ref, far_rows)]
    for k, out in enumerate(out_refs):
        if k > 0:
            note_ref, end = note_ends[k]
            notes = note_ref[end - SLOT_ROWS : end, :].astype(F32).astype(jnp.int32)
        if k == 1:
            out = out.at[far_rows:, :]
        for s in range(seqs):
            slot = slot_ref[s] if k == 0 else jnp.max(notes[s : s + 1, :])
            rows = pl.ds(pl.multiple_of(slot * tiles, 16), tiles)
            for g in range(groups):
                at = (g * seqs + s) * tiles
                out[at : at + tiles, :] = got_ref[g, rows, :]
        out[groups * seqs * tiles :, :] = table


def low_rank_kernel(
    tiles, place_ref, share_ref, codes_ref, adapt_refs, tokens_ref,
    low_ref, b4_ref, codes_t_ref, scr, held, table,
):
    n = len(adapt_refs)
    seqs = b4_ref.shape[0]
    groups = share_ref.shape[0]
    per_part = groups * seqs
    for k, part in enumerate(adapt_refs):
        part = part.at[part.shape[0] - per_part * (tiles + 1) :, :]
        table[k * per_part : (k + 1) * per_part, :] = part[per_part * tiles :, :].astype(F32)
        for g in range(groups):
            at = pl.multiple_of((g * n + (place_ref[0] ^ k)) * tiles, 16)
            for s in range(seqs):
                first = (g * seqs + s) * tiles
                held[s, pl.ds(at, tiles), :] = part[first : first + tiles, :]
    rows, tasks = table.shape[0], codes_ref.shape[0]
    task = table[:, :1].astype(jnp.int32)
    group = lax.broadcasted_iota(jnp.int32, (rows, 1), 0) % per_part // seqs
    for g in range(groups - 1):
        task = task + jnp.where(group > g, share_ref[g], 0)
    pick = (task == lax.broadcasted_iota(jnp.int32, (rows, tasks), 1)).astype(BF16)
    codes = dot(pick, codes_ref[...]).astype(BF16)
    at = lax.broadcasted_iota(jnp.int32, (rows, rows), 1)
    source = at % per_part // seqs * n + (place_ref[0] ^ (at // per_part))
    order = source * seqs + at % seqs == lax.broadcasted_iota(jnp.int32, (rows, rows), 0)
    codes_t_ref[...] = dot(order.astype(BF16), codes).T.astype(BF16)
    low_rank_body(held, tokens_ref, low_ref, b4_ref, scr)


def turn_tokens(tokens_ref, tok_t_ref):
    to = lax.broadcasted_iota(jnp.int32, (BLOCK_D, BLOCK_D), 0)
    sort = (
        to % BLOCK_Q * PACK + to // BLOCK_Q
        == lax.broadcasted_iota(jnp.int32, (BLOCK_D, BLOCK_D), 1)
    ).astype(BF16)
    for b in range(D // BLOCK_D):
        block = tokens_ref[:, b * BLOCK_D : (b + 1) * BLOCK_D]
        turned = dot_nt(sort, block).astype(BF16)
        for j in range(PACK):
            tok_t_ref[
                b * BLOCK_Q : (b + 1) * BLOCK_Q, j * block.shape[0] : (j + 1) * block.shape[0]
            ] = turned[j * BLOCK_Q : (j + 1) * BLOCK_Q, :]


def low_rank_body(adapt_ref, tokens_ref, low_ref, b4_ref, scr):
    seqs = b4_ref.shape[0]
    lane = lax.broadcasted_iota(jnp.int32, (BLOCK_D, LANES * seqs), 1)
    row = lax.broadcasted_iota(jnp.int32, (BLOCK_D, LANES * seqs), 0)
    keep = (lane % LANES) // R == row % PACK
    spread = (
        lax.broadcasted_iota(jnp.int32, (BLOCK_D, BLOCK_Q), 0) // PACK
        == lax.broadcasted_iota(jnp.int32, (BLOCK_D, BLOCK_Q), 1)
    ).astype(BF16)
    acc = jnp.zeros((tokens_ref.shape[0], LANES * seqs), F32)
    for b in range(D // BLOCK_D):
        cols = slice(b * BLOCK_D, (b + 1) * BLOCK_D)
        part = jnp.concatenate(
            [adapt_ref[s, b * BLOCK_Q : (b + 1) * BLOCK_Q, :] for s in range(seqs)], axis=1
        )
        wide = jnp.where(keep, dot(spread, part), 0.0).astype(BF16)
        block = tokens_ref[:, cols]
        acc = acc + dot(block, wide)
    first = lax.broadcasted_iota(jnp.int32, (SEQ_LEN, LANES), 1) < R
    for s in range(seqs):
        z = acc[s * SEQ_LEN : (s + 1) * SEQ_LEN, s * LANES : (s + 1) * LANES]
        total = z
        for j in range(1, PACK):
            total = total + pltpu.roll(z, j * R, 1)
        low_ref[s * SEQ_LEN : (s + 1) * SEQ_LEN, :] = jnp.where(first, total * SHRINK, 0.0).astype(
            BF16
        )
        scr[...] = adapt_ref[s, A_ROWS:, :].astype(F32)
        for c in range(COL_TILES):
            piece = scr[pl.ds(c, R, stride=COL_TILES), :].astype(BF16)
            for j in range(PACK):
                b4_ref[s, j * R : (j + 1) * R, c * LANES : (c + 1) * LANES] = piece


def frozen_kernel(n_tok, depth, own, layout, has_acc, packed, place_ref, *refs):
    refs = iter(refs)
    token_refs = [next(refs) for _ in range(n_tok)]
    weight_ref = next(refs) if own else None
    sets = [
        ([(m, next(refs)) for m in masks], segments) for masks, segments in layout
    ]
    accs = [next(refs) for _ in range(n_tok)] if has_acc else [None] * n_tok
    outs = list(refs)
    me, core, chip = place_ref[0], place_ref[1], place_ref[2]
    width = sets[0][0][0][1].shape[1]

    def cols(k, first, size):
        if packed:
            return slice((k - packed) * depth + first, (k - packed) * depth + first + size)
        return pl.ds(pl.multiple_of((me ^ k) * depth + first, LANES), size)

    for tok, acc, out in zip(token_refs, accs, outs):
        if own:
            half = out.shape[1]
            block = weight_ref[:, pl.ds(pl.multiple_of(core * half, LANES), half)]
            out[...] = dot(tok[:, cols(0, 0, depth)], block)
        else:
            out[...] = acc[...]
        for pieces, segments in sets:
            for first_chip in range(0, len(pieces), 2):
                pair = pieces[first_chip : first_chip + 2]
                part = None
                for k, first, size, row in segments:
                    right = jnp.concatenate([x[row : row + size, :] for _, x in pair], axis=1)
                    term = dot(tok[:, cols(k, first, size)], right)
                    part = term if part is None else part + term
                for at, (mask, _) in enumerate(pair):
                    where = pl.ds(pl.multiple_of((chip ^ mask) * width, LANES), width)
                    out[:, where] += part[:, at * width : (at + 1) * width]


def frozen_layout(sets):
    layout = [([m for m, _ in pieces], segments) for pieces, segments in sets]
    return layout, [x for pieces, _ in sets for _, x in pieces]


def frozen_call(place, depth, half, tokens, weight, sets, accs, packed=0):
    rows = tokens[0].shape[0]
    layout, flat = frozen_layout(sets)
    size = 2 * rows * sum(x.size for x in flat) + (0 if weight is None else 2 * rows * depth * half)
    weights = [] if weight is None else [weight]
    return call(
        functools.partial(
            frozen_kernel, len(tokens), depth, weight is not None, layout, bool(accs), packed
        ),
        [sds((rows, half), F32)] * len(tokens),
        n_smem=1,
        n_in=len(tokens) + len(weights) + len(flat) + len(accs),
        flops=size * len(tokens),
        nbytes=2 * sum(x.size for x in flat) + 4 * rows * half * len(tokens),
    )(place, *tokens, *weights, *flat, *accs)


def backward_kernel(
    loss_scale, place_ref, share_ref, slot_ref, counts_ref, mine_ref, theirs_ref, teacher_ref, low_ref, b4_ref, tok_t_ref, out_ref,
    values, spaced, grads,
):
    seqs = b4_ref.shape[0]
    half = mine_ref.shape[1]
    core, group = place_ref[1], place_ref[3]
    n_tasks = counts_ref.shape[0]
    first_task = jnp.int32(0)
    for g in range(share_ref.shape[0]):
        first_task = first_task + jnp.where(g < group, share_ref[g], 0)
    all_counts = counts_ref[0]
    for t in range(1, n_tasks):
        all_counts = all_counts + counts_ref[t]
    values[:, pl.ds(pl.multiple_of(core * half, LANES), half)] = mine_ref[...]
    values[:, pl.ds(pl.multiple_of((1 - core) * half, LANES), half)] = theirs_ref[...]
    blocks = []
    for s in range(seqs):
        rows = slice(s * SEQ_LEN, (s + 1) * SEQ_LEN)
        low = low_ref[rows, :]
        b4 = b4_ref[s]
        error = values[rows, :] + dot(low, b4) * RANK_SCALE - teacher_ref[rows, :].astype(F32)
        count = jnp.full((1, KV), counts_ref[first_task + slot_ref[s]], jnp.int32).astype(F32)
        mean = jnp.full((1, KV), all_counts, jnp.int32).astype(F32) / n_tasks
        value_grad = (error * (mean / count * loss_scale)).astype(BF16)
        blocks.append((dot_nt(value_grad, b4) * RANK_SCALE).astype(BF16))
        second = dot(low.T, value_grad)[:R] * RANK_SCALE
        for c in range(COL_TILES):
            spaced[pl.ds(c, R, stride=COL_TILES), :] = second[:, c * LANES : (c + 1) * LANES]
        grads[s, A_ROWS:, :] = spaced[...].astype(BF16)
    zero = jnp.zeros_like(blocks[0])
    low_grad = jnp.concatenate(
        [
            jnp.concatenate([blocks[s] if s == i else zero for i in range(seqs)], axis=1)
            for s in range(seqs)
        ],
        axis=0,
    )
    group = lax.broadcasted_iota(jnp.int32, low_grad.shape, 1) % LANES // R
    low_grad = jnp.concatenate(
        [jnp.where(group == j, low_grad, jnp.zeros_like(low_grad)) for j in range(PACK)], axis=0
    )
    first = (dot(tok_t_ref[...], low_grad) * SHRINK).astype(BF16)
    for s in range(seqs):
        grads[s, :A_ROWS, :] = first[:, s * LANES : (s + 1) * LANES]
    store_grads(grads, out_ref)


def store_grads(grads, out_ref):
    if len(out_ref.shape) == 3:
        out_ref[...] = grads[...]
        return
    tiles = out_ref.shape[2]
    for i in range(out_ref.shape[0]):
        for s in range(out_ref.shape[1]):
            out_ref[i, s] = grads[s, i * tiles : (i + 1) * tiles, :]


def hyper_kernel(step, codes_t_ref, grads_ref, out_ref, scr, done, sems):
    devices, seqs, tiles, _ = grads_ref.shape
    rows = devices * seqs
    for i in range(devices):
        for s in range(seqs):
            at = (i * seqs + s) * tiles
            scr[at : at + tiles, :] = grads_ref[i, s].astype(F32)
    codes_t = codes_t_ref[...]
    copies = []
    for k in range(tiles):
        part = scr[pl.ds(k, rows, stride=tiles), :].astype(BF16)
        done[:, k * LANES : (k + 1) * LANES] = dot(codes_t, part)
        if (k + 1) % step == 0:
            cols = slice((k + 1 - step) * LANES, (k + 1) * LANES)
            copies.append(
                pltpu.make_async_copy(done.at[:, cols], out_ref.at[:, cols], sems.at[k // step])
            )
            copies[-1].start()
    for copy in copies:
        copy.wait()


def tied(*groups):
    return lax.optimization_barrier(groups)


def shards(
    task_codes, hyper_weight, frozen_weight, tokens, teacher, seq_slot, task_share, token_counts
):
    groups = lax.axis_size("dp")
    members = lax.axis_size("mp")
    devices = groups * members
    chips = groups // 2
    tok_dev = tokens.shape[0]
    seqs = seq_slot.shape[0]
    depth = frozen_weight.shape[0]
    tiles = hyper_weight.shape[1] // LANES
    rows = A_ROWS + B_ROWS
    width_h = task_codes.shape[1]
    loss_scale = 1.0 / math.sqrt(tok_dev * members)
    me_dp, me_mp = lax.axis_index("dp"), lax.axis_index("mp")
    core, chip = me_dp % 2, me_dp // 2
    place = jnp.stack([me_mp, core, chip, me_dp]).astype(jnp.int32)
    half = KV // 2
    width = half // chips
    whole_tiles = tiles % 16 == 0

    mid = depth // 2

    def direct(block):
        return {
            m: xor_permute(block, "dp", m << 1) if m else block
            for m in range(chips)
            if m & (m - 1) == 0
        }

    def forwarded(held, by_high):
        held = dict(held)
        for m in range(1, chips):
            if m not in held:
                bit = 1 << (m.bit_length() - 1) if by_high else m & -m
                held[m] = xor_permute(held[m ^ bit], "dp", bit << 1)
        return held

    other_tokens = xor_permute(tokens, "dp", 1)
    fits = width % LANES == 0 and mid % LANES == 0 and members == 4 and chips == 4
    fits = fits and whole_tiles and groups * seqs % 16 == 0
    near_rows = [(1, 0, depth, 0)]
    if fits:
        near, top, bottom = pl.pallas_call(
            chunk_kernel,
            in_specs=[pl.BlockSpec(memory_space=pltpu.SMEM)]
            + [pl.BlockSpec(memory_space=pltpu.HBM)] * 2,
            out_specs=[pl.BlockSpec(memory_space=pltpu.VMEM)] * 3,
            out_shape=[sds((n + SLOT_ROWS, width), BF16) for n in (depth, mid, mid)],
            scratch_shapes=[
                pltpu.SMEM(seq_slot.shape, jnp.int32),
                pltpu.SemaphoreType.DMA((4,)),
            ],
            compiler_params=pltpu.CompilerParams(vmem_limit_bytes=ALL_VMEM),
        )(place, seq_slot, frozen_weight)
        near, top, bottom, task_codes = tied(near, top, bottom, task_codes)
        other_tokens, task_codes = tied(other_tokens, task_codes)
        near = xor_permute(near, "mp", 1)
        top = xor_permute(top, "mp", 2)
        bottom = xor_permute(bottom, "mp", 3)
        near_held = direct(near)
        far = jnp.concatenate([top, bottom], axis=0)
        at = mid + SLOT_ROWS
        far_rows = [(2, 0, mid, 0), (3, mid, mid, at)]
        third_rows = [(3, 0, mid, 0), (2, mid, mid, at)]
    else:
        chunk = lax.dynamic_slice_in_dim(frozen_weight, core * half + chip * width, width, 1)
        near = xor_permute(chunk, "mp", 1)
        near_held = direct(near)
        far = jnp.concatenate(
            [xor_permute(chunk, "mp", k) for k in range(2, members)], axis=0
        )
        far_rows = [(k, 0, depth, (k - 2) * depth) for k in range(2, members)]

    if fits:
        sent = call(
            functools.partial(adapters_kernel, tiles),
            [sds((groups, TPG * tiles + SLOT_ROWS, LANES), BF16)],
            scratch=[pltpu.VMEM((groups * TPG * tiles, LANES), F32)],
            n_smem=2,
            n_in=2,
            flops=2 * groups * TPG * hyper_weight.size,
            nbytes=4 * hyper_weight.size,
        )(task_share, seq_slot, task_codes, hyper_weight)[0]
        got = lax.all_to_all(sent, "dp", 0, 0, tiled=True)
        chosen = call(
            functools.partial(choose_kernel, tiles),
            [
                sds((groups * seqs * (tiles + 1) + (far.shape[0] if k == 1 else 0), LANES), BF16)
                for k in range(members)
            ],
            n_smem=1,
            n_in=3,
            nbytes=8 * hyper_weight.size,
        )(seq_slot, near, far, got)
        near_held, far, chosen = tied(near_held, far, chosen)
        near_pieces = forwarded(near_held, True)
        adapt = [chosen[0]] + [xor_permute(chosen[k], "mp", k) for k in range(1, members)]
        third = adapt[1][: far.shape[0]]
    else:
        near_pieces = forwarded(near_held, True)
        slots = lax.all_to_all(
            jnp.broadcast_to(seq_slot[None], (devices, seqs)), ("dp", "mp"), 0, 0, tiled=True
        ).reshape(-1)
        offsets = jnp.cumsum(task_share) - task_share
        task_of = jnp.repeat(offsets, members * seqs) + slots
        pick = (jnp.arange(task_codes.shape[0])[:, None] == task_of[None, :]).astype(BF16)
        codes_t = dot(task_codes.T, pick).astype(BF16)
        sent = dot(codes_t.T, hyper_weight).astype(BF16).reshape(devices, seqs, tiles, LANES)
        adapt = lax.all_to_all(sent, ("dp", "mp"), 0, 0, tiled=True)
        adapt = adapt.transpose(1, 0, 2, 3).reshape(seqs, rows, LANES)

    low_outs = [
        sds((tok_dev, LANES), BF16),
        sds((seqs, LANES, KV), BF16),
    ]
    turned = sds((D // PACK, PACK * tok_dev), BF16)
    far_held = direct(far)
    if fits:
        sets = [(list(near_held.items()), near_rows)]
        early_layout, flat = frozen_layout(sets)

        def early(place_ref, *refs):
            *refs, tok_t_ref = refs
            turn_tokens(refs[0], tok_t_ref)
            frozen_kernel(2, depth, True, early_layout, False, 0, place_ref, *refs)

        *accs, tok_t = call(
            early,
            [sds((tok_dev, half), F32)] * 2 + [turned],
            n_smem=1,
            n_in=3 + len(flat),
        )(place, tokens, other_tokens, frozen_weight, *flat)
        last = chips - 1
        third, accs, near_last = tied(third, accs, near_pieces[last])
        third_held = direct(third)
        third_held, far_held, accs, adapt = tied(third_held, far_held, accs, adapt)
        third_pieces = forwarded(third_held, True)
    far_pieces = forwarded(far_held, False)

    low_cost = dict(
        flops=4 * tokens.size * LANES * seqs, nbytes=4 * tokens.size + 4 * seqs * rows * LANES
    )
    low_scratch = [pltpu.VMEM((B_ROWS, LANES), F32)]
    if fits:
        last = chips - 1
        sets = [
            ([(last, near_last)], near_rows),
            ([(m, far_held[m]) for m in far_held], far_rows),
            ([(m, third_held[m]) for m in third_held], third_rows),
        ]
        layout, flat = frozen_layout(sets)
        n_flat, n_adapt = len(flat), len(adapt)

        def middle(*refs):
            refs = list(refs)
            place_ref, share_ref, codes_ref = refs[:3]
            token_refs, refs = refs[3:5], refs[5:]
            piece_refs, refs = refs[:n_flat], refs[n_flat:]
            acc_refs, refs = refs[:2], refs[2:]
            adapt_refs, refs = refs[:n_adapt], refs[n_adapt:]
            out_refs, late_ref, refs = refs[:2], refs[2], refs[3:]
            for k in range(2, members):
                block = pl.ds(pl.multiple_of((place_ref[0] ^ k) * depth, LANES), depth)
                late_ref[:, (k - 2) * depth : (k - 1) * depth] = token_refs[1][:, block]
            low_rank_kernel(
                tiles, place_ref, share_ref, codes_ref, adapt_refs, token_refs[0], *refs
            )
            frozen_kernel(
                2, depth, False, layout, True, 0, place_ref, *token_refs, *piece_refs, *acc_refs,
                *out_refs,
            )

        *accs, late_tokens, low, b4, codes_t = call(
            middle,
            [sds((tok_dev, half), F32)] * 2
            + [sds((tok_dev, (members - 2) * depth), BF16)]
            + low_outs
            + [sds((width_h, devices * seqs), BF16)],
            scratch=low_scratch
            + [
                pltpu.VMEM((seqs, rows, LANES), BF16),
                pltpu.VMEM((devices * seqs, LANES), F32),
            ],
            n_smem=2,
            n_in=5 + n_flat + n_adapt,
        )(place, task_share, task_codes, tokens, other_tokens, *flat, *accs, *adapt)
        sets = [([(last, far_pieces[last])], far_rows), ([(last, third_pieces[last])], third_rows)]
        theirs = frozen_call(place, depth, half, [late_tokens], None, sets, accs[1:], 2)[0]
        mine = frozen_call(place, depth, half, [tokens], None, sets, accs[:1])[0]
    else:
        low, b4 = call(low_rank_body, low_outs, scratch=low_scratch, n_in=2, **low_cost)(
            adapt, tokens
        )
        tok_t = call(turn_tokens, [turned], n_in=1)(tokens)[0]
        own_half = lax.dynamic_slice_in_dim(frozen_weight, core * half, half, 1)
        order = jnp.arange(chips) ^ chip
        found = {0: own_half}
        for pieces, segments in ((near_pieces, near_rows), (far_pieces, far_rows)):
            joined = jnp.stack([pieces[m] for m in range(chips)])
            joined = jnp.take(joined, order, axis=0).transpose(1, 0, 2).reshape(-1, half)
            for k, _, size, row in segments:
                found[k] = joined[row : row + size]
        blocks = jnp.stack([found[k] for k in range(members)])
        weight = jnp.take(blocks, jnp.arange(members) ^ me_mp, axis=0).reshape(D, half)
        mine = jnp.dot(tokens, weight, preferred_element_type=F32)
        theirs = jnp.dot(other_tokens, weight, preferred_element_type=F32)
    received = xor_permute(theirs, "dp", 1)

    split = (devices, seqs, tiles, LANES)
    grads = call(
        functools.partial(backward_kernel, loss_scale),
        [sds(split if whole_tiles else (seqs, rows, LANES), BF16)],
        scratch=[
            pltpu.VMEM((tok_dev, KV), F32),
            pltpu.VMEM((B_ROWS, LANES), F32),
            pltpu.VMEM((seqs, rows, LANES), BF16),
        ],
        n_smem=4,
        n_in=6,
        flops=4 * tokens.size * LANES * seqs,
        nbytes=4 * tokens.size,
    )(place, task_share, seq_slot, token_counts, mine, received, teacher, low, b4, tok_t)[0]
    if not whole_tiles:
        grads = grads.reshape(seqs, devices, tiles, LANES).transpose(1, 0, 2, 3)
    routed = lax.all_to_all(grads, ("dp", "mp"), 0, 0, tiled=True)
    step = 4 if whole_tiles else tiles
    return pl.pallas_call(
        functools.partial(hyper_kernel, step),
        out_shape=sds((width_h, tiles * LANES), F32),
        in_specs=[pl.BlockSpec(memory_space=pltpu.VMEM)] * 2,
        out_specs=pl.BlockSpec(memory_space=pl.ANY),
        scratch_shapes=[
            pltpu.VMEM((devices * seqs * tiles, LANES), F32),
            pltpu.VMEM((width_h, tiles * LANES), F32),
            pltpu.SemaphoreType.DMA((tiles // step,)),
        ],
        compiler_params=pltpu.CompilerParams(vmem_limit_bytes=VMEM_LIMIT),
    )(codes_t, routed)


def solution(mesh):
    placed = (
        P(),
        P(None, ("dp", "mp")),
        P("mp", None),
        P(("dp", "mp"), None),
        P(("dp", "mp"), None),
        P(("dp", "mp")),
        P(),
        P(),
    )
    return jax.shard_map(
        shards, mesh=mesh, in_specs=placed, out_specs=P(None, ("dp", "mp")), check_vma=False
    )
```
